32 devices in a mesh: tm: 4 (over y, x), sx: 2 (over core), sy: 4 (over z).
Axes of the slice: x: 2, y: 2, z: 4, core: 2. Of those that a mesh axis runs over, the one named last changes fastest.
Arguments:
- initial: float32 [512, 2048], P('sx', 'sy'), may hold values from 0.5 to 1.5
- kappa: float32 [512, 2048], P('sx', 'sy'), may hold values from 0.0016 to 0.016
- c_guess: float32 [4, 512, 2048], P('tm', 'sx', 'sy'), may hold values from 0.5 to 1.5
Outputs:
- c_values: float32 [4, 512, 2048], P('tm', 'sx', 'sy')
- f_values: float32 [4, 512, 2048], P('tm', 'sx', 'sy')
The draws below stay inside these ranges and needn't reach their ends.
All inputs are finite; a program needn't handle non-finite values.
Results may differ from the reference program's by a relative error of at most 0.00002.
Values sent between devices are 32-bit elements; how exact they have to be, the bound alone decides.
No kernel may reach another device: no remote copies, remote signals or barrier semaphores. Data moves between devices by JAX's collectives and lax.ppermute only.
A program may use at most 64 MiB of HBM per device.

```python
import math
import jax
import jax.numpy as jnp

NT1 = 4
NT2 = 2
NX = 512
NY = 2048


def shard_levels(stream_key, extent, split, least, high):
    gain = 1.0
    for dim, shards_of in split:
        draws = jax.random.uniform(jax.random.fold_in(jax.random.fold_in(stream_key, 6), dim), (shards_of,), jnp.float32, least / len(split), high / len(split))
        gain = gain * jnp.repeat(jnp.exp(draws), extent[dim] // shards_of).reshape((-1,) + (1,) * (len(extent) - 1 - dim))
    return gain


def setup_inputs(seed: int = 0) -> dict:
    key_list = jax.random.split(jax.random.key(seed), 4)
    initial = jnp.clip(0.5 + 1.0 * jax.random.uniform(key_list[0], (NX, NY), jnp.float32) ** shard_levels(key_list[0], (NX, NY), ((0, 2), (1, 4)), -0.2, 0.2), 0.5, 1.5)
    kappa = jnp.clip(jnp.exp(math.log(0.016) - 2.3025852 * jax.random.uniform(key_list[1], (NX, NY), jnp.float32) ** shard_levels(key_list[1], (NX, NY), ((0, 2), (1, 4)), -0.2, 0.2)), 0.0016, 0.016)
    c_guess = jnp.clip(0.5 + 1.0 * jax.random.uniform(key_list[2], (NT1, NX, NY), jnp.float32) ** shard_levels(key_list[2], (NT1, NX, NY), ((0, 4), (1, 2), (2, 4)), -0.2, 0.2), 0.5, 1.5)
    return dict(initial=initial, kappa=kappa, c_guess=c_guess)


def spread(field, kappa):
    flux = kappa * field * field
    widths = [(0, 0)] * (flux.ndim - 2) + [(1, 1), (1, 1)]
    padded = jnp.pad(flux, widths)
    return padded[..., 2:, 1:-1] + padded[..., :-2, 1:-1] + padded[..., 1:-1, 2:] + padded[..., 1:-1, :-2] - 4.0 * flux


def reference(initial, kappa, c_guess):
    prev_w = jnp.concatenate([initial[None], c_guess[:-1]], axis=0)
    lap_w = spread(prev_w, kappa)
    fine = prev_w + lap_w
    lap_f = spread(fine, kappa)
    value = fine + lap_f
    first_rhs = value - prev_w - 2.0 * lap_w
    quarter = prev_w + 4.0 * lap_w
    value_odd = value[0::2]
    second_rhs = value_odd + 2.0 * spread(value_odd, kappa) + first_rhs[1::2] - quarter[0::2]
    state = initial
    states = [initial]
    for level in range(NT2):
        state = state + 4.0 * spread(state, kappa) + second_rhs[level]
        states.append(state)
    coarse = jnp.stack(states)
    lower = coarse[:-1]
    even_part = lower + 2.0 * spread(lower, kappa) + first_rhs[0::2]
    odd_part = coarse[1:]
    c_values = jnp.stack([even_part, odd_part], axis=1).reshape(NT1, NX, NY)
    prev_n = jnp.concatenate([initial[None], c_values[:-1]], axis=0)
    f_values = prev_n + spread(prev_n, kappa)
    return c_values, f_values
```

```python
import functools
import jax
import jax.numpy as jnp
from jax import lax
from jax.experimental import pallas as pl
from jax.experimental.pallas import tpu as pltpu
from jax.sharding import PartitionSpec as P

LANES = 128
SUBLANES = 8
VMEM = pltpu.VMEM


def round_up(value, step):
    return -(-value // step) * step


def ring_pairs(order):
    size = len(order)
    return [(order[i], order[(i + 1) % size]) for i in range(size)]


def both_ways(axis, gray=False):
    size = lax.axis_size(axis)
    order = list(range(size))
    if gray and size & (size - 1) == 0:
        order = [i ^ (i >> 1) for i in order]
    ahead = ring_pairs(order)
    return ahead, [(j, i) for i, j in ahead], order


def edge_kernel(halo, rows, rows_before, rows_after, *refs):
    fields = len(refs) // 2 - 1
    lefts, rights = refs[:fields], refs[fields : 2 * fields]
    first_out, last_out = refs[2 * fields :]
    ix, last_ix = lax.axis_index("sx"), lax.axis_size("sx") - 1
    length = first_out.shape[-1]
    width = rows_before.shape[-1]
    for k in range(fields):
        for block, out, col, lo in (
            (lefts[k], first_out, 0, 0),
            (rights[k], last_out, width - LANES, LANES - halo),
        ):
            after = rows_after[k, :, col : col + LANES]
            before = rows_before[k, :, col : col + LANES]
            if k == 0:
                after = jnp.where(ix == last_ix, 0.0, after)
                before = jnp.where(ix == 0, 0.0, before)
            rest = jnp.zeros((length - rows - 2 * halo, LANES), jnp.float32)
            whole = jnp.concatenate([block[...], after, before, rest], axis=0)
            out[k] = whole.T[lo : lo + halo]


def solve_kernel(plan, *refs):
    rows, width, halo, count, position = (
        plan["rows"], plan["width"], plan["halo"], plan["count"], plan["position"],
    )
    names = plan["names"]
    ref = dict(zip(names, refs))
    kap, state, mid, lap_w, wk, first, second, fa, fb = refs[len(names) + 2 :]
    c_out, f_out = refs[len(names) : len(names) + 2]
    total, wide = rows + 2 * halo, width + LANES
    here = lax.axis_index("tm")
    ix, last_ix = lax.axis_index("sx"), lax.axis_size("sx") - 1
    iy, last_iy = lax.axis_index("sy"), lax.axis_size("sy") - 1
    blocks = total // SUBLANES

    def fill(dst, tile, before, after, left, right, mask=False):
        dst[0:rows, 0:width] = tile
        if mask:
            after = jnp.where(ix == last_ix, 0.0, after)
            before = jnp.where(ix == 0, 0.0, before)
            right = jnp.where(iy == last_iy, 0.0, right)
            left = jnp.where(iy == 0, 0.0, left)
        dst[rows : rows + halo, 0:width] = after
        dst[rows + halo : total, 0:width] = before
        gap = jnp.zeros((LANES - 2 * halo, left.shape[-1]), jnp.float32)
        sides = jnp.concatenate([right, gap, left], axis=0).T
        dst[:, width:wide] = sides[:total]

    def at(i):
        return pl.ds(pl.multiple_of(i * SUBLANES, SUBLANES), SUBLANES)

    def flux_at(dst, i, value):
        dst[at(i + 1), :] = value

        @pl.when(i == 0)
        def _():
            dst[at(blocks + 1), :] = value

        @pl.when(i == blocks - 1)
        def _():
            dst[at(0), :] = value

    def over(body):
        def step(i, carry):
            body(i)
            return carry

        lax.fori_loop(0, blocks, step, 0)

    row = lax.broadcasted_iota(jnp.int32, (SUBLANES, wide), 0)

    def lap(src, i):
        low, cur, high = src[at(i), :], src[at(i + 1), :], src[at(i + 2), :]
        up = jnp.where(row == 0, pltpu.roll(low, 1, 0), pltpu.roll(cur, 1, 0))
        down = jnp.where(row == SUBLANES - 1, pltpu.roll(high, SUBLANES - 1, 0), pltpu.roll(cur, SUBLANES - 1, 0))
        return down + up + pltpu.roll(cur, wide - 1, 1) + pltpu.roll(cur, 1, 1) - 4.0 * cur

    def flux(dst, src):
        def body(i):
            v = src[at(i), :]
            flux_at(dst, i, kap[at(i), :] * v * v)

        over(body)

    def first_part(w, g):
        flux(fa, w)

        def one(i):
            lw = lap(fa, i)
            lap_w[at(i), :] = lw
            f = w[at(i), :] + lw
            mid[at(i), :] = f
            flux_at(fb, i, kap[at(i), :] * f * f)

        over(one)

        def two(i):
            v = mid[at(i), :] + lap(fb, i)
            mid[at(i), :] = v
            g[at(i), :] = (v - w[at(i), :]) - 2.0 * lap_w[at(i), :]
            flux_at(fa, i, kap[at(i), :] * v * v)

        over(two)

    def second_part(w, g):
        def one(i):
            v = mid[at(i), :]
            q = w[at(i), :] + 4.0 * lap_w[at(i), :]
            g[at(i), :] = v + 2.0 * lap(fa, i) - q

        over(one)

    def load(point):
        if point < 0:
            fill(wk, ref["initial"][...], ref["before"][1], ref["after"][1], ref["left"][1], ref["right"][1])
            return
        mine = jnp.int32(0)
        theirs = position[point]
        for t in range(count):
            mine = jnp.where(here == t, position[t], mine)
        away = lax.rem(mine - theirs + count, count)
        for s in range(1, count):

            @pl.when(away == s)
            def _():
                if 2 * s == count:
                    tile = jnp.concatenate([ref["half_back"][0], ref["half_ahead"][0]], axis=0)
                else:
                    tile = ref[f"tile_{s}"][0]
                strips = ref[f"strip_{s}"]
                side = strips.shape[-1] - width
                fill(
                    wk, tile,
                    strips[:halo, :width], strips[halo:, :width],
                    strips[:halo, width:], strips[halo:, width:],
                )

    fill(kap, ref["kappa"][...], ref["before"][0], ref["after"][0], ref["left"][0], ref["right"][0], True)
    fill(state, ref["initial"][...], ref["before"][1], ref["after"][1], ref["left"][1], ref["right"][1])

    inner = rows // SUBLANES

    def tail(j):
        load(2 * j - 1)
        first_part(wk, first)

        @pl.when(lax.rem(here, 2) == 1)
        def _():
            second_part(wk, second)

        flux(fb, state)

        @pl.when(lax.rem(here, 2) == 0)
        def _():
            def body(i):
                x, lx = state[at(i), :], lap(fb, i)
                c = x + 2.0 * lx + first[at(i), :]

                @pl.when(i < inner)
                def _():
                    c_out[0, at(i), :] = c[:, :width]
                    f_out[0, at(i), :] = (x + lx)[:, :width]

            over(body)

        @pl.when(lax.rem(here, 2) == 1)
        def _():
            def body(i):
                x, lx = state[at(i), :], lap(fb, i)
                c = x + 2.0 * lx + first[at(i), :]
                mid[at(i), :] = c
                flux_at(fa, i, kap[at(i), :] * c * c)
                second[at(i), :] = x + 4.0 * lx + second[at(i), :]

            over(body)

            def last(i):
                @pl.when(i < inner)
                def _():
                    f_out[0, at(i), :] = (mid[at(i), :] + lap(fa, i))[:, :width]

            over(last)
            load(2 * j)
            first_part(wk, first)

            def add(i):
                @pl.when(i < inner)
                def _():
                    c_out[0, at(i), :] = (second[at(i), :] + first[at(i), :])[:, :width]

            over(add)

    for j in range((count + 1) // 2):

        @pl.when(lax.div(here, 2) == j)
        def _():
            tail(j)

        if 2 * j + 2 < count:

            @pl.when(lax.div(here, 2) > j)
            def _():
                load(2 * j - 1)
                first_part(wk, first)
                second_part(wk, second)
                load(2 * j)
                first_part(wk, first)
                flux(fb, state)

                def body(i):
                    state[at(i), :] = state[at(i), :] + 4.0 * lap(fb, i) + (second[at(i), :] + first[at(i), :])

                over(body)


def on_device(initial, kappa, c_guess):
    count = lax.axis_size("tm")
    rows, width = initial.shape
    halo = round_up(count // 2 + 3, SUBLANES)
    total, wide = rows + 2 * halo, width + LANES
    ahead, back, order = both_ways("tm", gray=True)
    position = [order.index(t) for t in range(count)]
    middle = rows // 2

    def kernel(body, outs, scratch=()):
        return pl.pallas_call(
            body,
            out_shape=[jax.ShapeDtypeStruct(s, jnp.float32) for s in outs],
            scratch_shapes=[VMEM(s, jnp.float32) for s in scratch],
            compiler_params=pltpu.CompilerParams(vmem_limit_bytes=48 * 2**20),
        )

    tiles = {}
    onward, backward = c_guess, c_guess
    for s in range(1, count // 2):
        onward = lax.ppermute(onward, "tm", ahead)
        backward = lax.ppermute(backward, "tm", back)
        tiles[s], tiles[count - s] = onward, backward
    half_ahead = lax.ppermute(onward[:, middle:], "tm", ahead)
    half_back = lax.ppermute(backward[:, :middle], "tm", back)

    sx_up, sx_down, _ = both_ways("sx")
    sy_up, sy_down, _ = both_ways("sy")
    fields = (kappa, initial, c_guess[0])
    before = lax.ppermute(jnp.stack([x[rows - halo :] for x in fields]), "sx", sx_up)
    after = lax.ppermute(jnp.stack([x[:halo] for x in fields]), "sx", sx_down)
    length = round_up(total, LANES)
    packed = (len(fields), halo, length)
    first_cols, last_cols = kernel(functools.partial(edge_kernel, halo, rows), [packed] * 2)(
        before, after, *[x[:, :LANES] for x in fields], *[x[:, width - LANES :] for x in fields]
    )
    left = lax.ppermute(last_cols, "sy", sy_up)
    right = lax.ppermute(first_cols, "sy", sy_down)

    strip = jnp.concatenate(
        [jnp.concatenate([before[2], after[2]], axis=0), jnp.concatenate([left[2], right[2]], axis=0)], axis=1
    )
    strips = {}
    onward, backward = strip, strip
    for s in range(1, count // 2 + 1):
        onward = lax.ppermute(onward, "tm", ahead)
        strips[s] = onward
        if 2 * s < count:
            backward = lax.ppermute(backward, "tm", back)
            strips[count - s] = backward

    given = dict(
        kappa=kappa, initial=initial, before=before, after=after, left=left, right=right,
        half_ahead=half_ahead, half_back=half_back,
    )
    given |= {f"tile_{s}": x for s, x in tiles.items()}
    given |= {f"strip_{s}": x for s, x in strips.items()}
    plan = dict(rows=rows, width=width, halo=halo, count=count, position=position, names=list(given))
    ext = (total, wide)
    padded = (total + 2 * SUBLANES, wide)
    c_new, f_new = kernel(
        functools.partial(solve_kernel, plan), [c_guess.shape] * 2, [ext] * 7 + [padded] * 2
    )(*given.values())
    return c_new, f_new


def solution(mesh):
    return jax.shard_map(
        on_device,
        mesh=mesh,
        in_specs=(P("sx", "sy"), P("sx", "sy"), P("tm", "sx", "sy")),
        out_specs=(P("tm", "sx", "sy"), P("tm", "sx", "sy")),
        check_vma=False,
    )
```

```python
import functools
import jax
import jax.numpy as jnp
from jax import lax
from jax.experimental import pallas as pl
from jax.experimental.pallas import tpu as pltpu
from jax.sharding import PartitionSpec as P

LANES = 128
SUBLANES = 8
BLOCK = 16


def round_up(value, step):
    return -(-value // step) * step


def ring(axis, gray=False):
    size = lax.axis_size(axis)
    order = list(range(size))
    if gray and size & (size - 1) == 0:
        order = [i ^ (i >> 1) for i in order]
    return order


def shift(x, axis, order, by):
    size = len(order)
    return lax.ppermute(x, axis, [(order[i], order[(i + by) % size]) for i in range(size)])


def call(body, outs, scratch=(), **options):
    return pl.pallas_call(
        body,
        out_shape=[jax.ShapeDtypeStruct(s, jnp.float32) for s in outs],
        scratch_shapes=[pltpu.VMEM(s, jnp.float32) for s in scratch],
        compiler_params=pltpu.CompilerParams(vmem_limit_bytes=48 * 2**20),
        **options,
    )


def edge_kernel(halo, rows, rows_before, rows_after, *refs):
    fields = len(refs) // 2 - 1
    lefts, rights = refs[:fields], refs[fields : 2 * fields]
    first_out, last_out = refs[2 * fields :]
    ix, last_ix = lax.axis_index("sx"), lax.axis_size("sx") - 1
    length = first_out.shape[-1]
    width = rows_before.shape[-1]
    for k in range(fields):
        for block, out, col, lo in (
            (lefts[k], first_out, 0, 0),
            (rights[k], last_out, width - LANES, LANES - halo),
        ):
            after = rows_after[k, :, col : col + LANES]
            before = rows_before[k, :, col : col + LANES]
            if k == 0:
                after = jnp.where(ix == last_ix, 0.0, after)
                before = jnp.where(ix == 0, 0.0, before)
            rest = jnp.zeros((length - rows - 2 * halo, LANES), jnp.float32)
            whole = jnp.concatenate([block[...], after, before, rest], axis=0)
            out[k] = whole.T[lo : lo + halo]


class Grid:
    def __init__(self, rows, width, halo):
        self.rows, self.width, self.halo = rows, width, halo
        self.total, self.wide = rows + 2 * halo, width + LANES
        self.ext = (self.total, self.wide)
        self.padded = (self.total + 2 * SUBLANES, self.wide)

    def fill(self, dst, tile, before, after, left, right):
        rows, halo, total, width = self.rows, self.halo, self.total, self.width
        at = 0
        for part in tile:
            dst[at : at + part.shape[0], 0:width] = part
            at += part.shape[0]
        dst[rows : rows + halo, 0:width] = after
        dst[rows + halo : total, 0:width] = before
        gap = jnp.zeros((LANES - 2 * halo, left.shape[-1]), jnp.float32)
        sides = jnp.concatenate([right, gap, left], axis=0).T
        dst[:, width:] = sides[:total]

    def over(self, body, dst=None):
        total = self.total
        for o in range(0, total, BLOCK):
            size = min(BLOCK, total - o)
            value = body(slice(o, o + size))
            if dst is None:
                continue
            dst[o + SUBLANES : o + SUBLANES + size, :] = value
            if o == 0:
                dst[total + SUBLANES :, :] = value[:SUBLANES]
            if o + size == total:
                dst[0:SUBLANES, :] = value[size - SUBLANES :]

    def lap(self, src, at):
        size, wide = at.stop - at.start, self.wide
        around = src[at.start : at.stop + 2 * SUBLANES, :]
        cur = around[SUBLANES : SUBLANES + size]
        up = pltpu.roll(around, 1, 0)[SUBLANES : SUBLANES + size]
        down = pltpu.roll(around, size + 2 * SUBLANES - 1, 0)[SUBLANES : SUBLANES + size]
        return down + up + pltpu.roll(cur, wide - 1, 1) + pltpu.roll(cur, 1, 1) - 4.0 * cur

    def flux(self, kap, src, dst):
        def body(at):
            v = src[at, :]
            return kap[at, :] * v * v

        self.over(body, dst)

    def first_part(self, kap, w, mid, lap_w, fa, fb, out):
        self.flux(kap, w, fa)

        def one(at):
            lw = self.lap(fa, at)
            lap_w[at, :] = lw
            f = w[at, :] + lw
            mid[at, :] = f
            return kap[at, :] * f * f

        self.over(one, fb)

        def two(at):
            v = mid[at, :] + self.lap(fb, at)
            mid[at, :] = v
            out(at, (v - w[at, :]) - 2.0 * lap_w[at, :])
            return kap[at, :] * v * v

        self.over(two, fa)

    def second_part(self, w, mid, lap_w, fa, out):
        def one(at):
            q = w[at, :] + 4.0 * lap_w[at, :]
            out(at, mid[at, :] + 2.0 * self.lap(fa, at) - q)

        self.over(one)


def absorb(grid, kap, point, here, load, even, odd, tail, work):
    wk, mid, lap_w, fa, fb = work
    load(wk)
    step = lax.div(point, 2)

    @pl.when(lax.rem(point, 2) == 1)
    def _():
        def out(at, g):
            odd[step, at, :] = g

        grid.first_part(kap, wk, mid, lap_w, fa, fb, out)

    @pl.when(lax.rem(point, 2) == 0)
    def _():
        def out(at, g):
            tail[at, :] = g

        grid.first_part(kap, wk, mid, lap_w, fa, fb, out)

        @pl.when(point < here)
        def _():
            def out(at, h):
                even[step, at, :] = h

            grid.second_part(wk, mid, lap_w, fa, out)


def start_kernel(grid, kappa, initial, before, after, left, right, kap, even, tail, low, wk, mid, lap_w, fa, fb):
    ix, last_ix = lax.axis_index("sx"), lax.axis_size("sx") - 1
    iy, last_iy = lax.axis_index("sy"), lax.axis_size("sy") - 1
    grid.fill(
        kap, [kappa[...]],
        jnp.where(ix == 0, 0.0, before[0]), jnp.where(ix == last_ix, 0.0, after[0]),
        jnp.where(iy == 0, 0.0, left[0]), jnp.where(iy == last_iy, 0.0, right[0]),
    )
    grid.fill(wk, [initial[...]], before[1], after[1], left[1], right[1])

    def out(at, g):
        x, lx = wk[at, :], lap_w[at, :]
        tail[at, :] = x + 2.0 * lx + g
        low[at, :] = x + lx

    grid.first_part(kap, wk, mid, lap_w, fa, fb, out)

    def out_even(at, h):
        even[0, at, :] = (wk[at, :] + 4.0 * lap_w[at, :]) + h

    grid.second_part(wk, mid, lap_w, fa, out_even)


def arrival(grid, index, away, tile, strip, kap, here_pos, order, even, odd, tail, work):
    count = len(order)
    here, point = lax.axis_index("tm"), jnp.int32(count)
    for p in range(count):
        point = jnp.where(here == order[p], order[(p - away) % count] + 1, point)

    def load(wk):
        halo, width = grid.halo, grid.width
        strips = strip[...]
        grid.fill(
            wk, [t[0] for t in tile],
            strips[:halo, :width], strips[halo:, :width], strips[:halo, width:], strips[halo:, width:],
        )

    @pl.when(point <= here)
    def _():
        absorb(grid, kap, point, here, load, even, odd, tail, work)


def middle_kernel(grid, order, aways, kap, even_in, odd_in, tail_in, *refs):
    pairs = [refs[2 * i : 2 * i + 2] for i in range(len(aways))]
    even, odd, tail = refs[2 * len(aways) : 2 * len(aways) + 3]
    work = refs[2 * len(aways) + 3 :]
    for away, (tile, strip) in zip(aways, pairs):
        arrival(grid, None, away, [tile], strip, kap, None, order, even, odd, tail, work)


def last_kernel(grid, order, kap, even, odd_in, tail_in, low, first, second, strip, c_out, f_out, odd, tail, *work):
    wk, mid, lap_w, fa, fb = work
    count = len(order)
    here = lax.axis_index("tm")
    rows, width = grid.rows, grid.width
    if count > 1:
        arrival(grid, None, count // 2, [first, second], strip, kap, None, order, even, odd, tail, work)
    state = wk

    def put(dst, at, value):
        stop = min(at.stop, rows)
        if at.start < stop:
            dst[0, at.start : stop, :] = value[: stop - at.start, :width]

    @pl.when(here == 0)
    def _():
        c_out[0] = tail[:rows, :width]
        f_out[0] = low[:rows, :width]

    @pl.when(here == 1)
    def _():
        grid.flux(kap, tail, fa)

        def body(at):
            put(c_out, at, even[0, at, :] + odd[0, at, :])
            put(f_out, at, tail[at, :] + grid.lap(fa, at))

        grid.over(body)

    @pl.when(here >= 2)
    def _():
        def begin(at):
            x = even[0, at, :] + odd[0, at, :]
            state[at, :] = x
            return kap[at, :] * x * x

        grid.over(begin, fb)

        if count > 4:

            def step(j, carry):
                def body(at):
                    x = state[at, :] + 4.0 * grid.lap(fb, at) + (even[j, at, :] + odd[j, at, :])
                    state[at, :] = x
                    return kap[at, :] * x * x

                grid.over(body, fa)
                fb[...] = fa[...]
                return carry

            lax.fori_loop(1, lax.div(here, 2), step, 0)

        @pl.when(lax.rem(here, 2) == 0)
        def _():
            def body(at):
                x, lx = state[at, :], grid.lap(fb, at)
                put(c_out, at, x + 2.0 * lx + tail[at, :])
                put(f_out, at, x + lx)

            grid.over(body)

        @pl.when(lax.rem(here, 2) == 1)
        def _():
            j = lax.div(here, 2)

            def body(at):
                x, lx = state[at, :], grid.lap(fb, at)
                c = x + 2.0 * lx + tail[at, :]
                mid[at, :] = c
                put(c_out, at, x + 4.0 * lx + (even[j, at, :] + odd[j, at, :]))
                return kap[at, :] * c * c

            grid.over(body, fa)

            def last(at):
                put(f_out, at, mid[at, :] + grid.lap(fa, at))

            grid.over(last)


def on_device(initial, kappa, c_guess):
    count = lax.axis_size("tm")
    rows, width = initial.shape
    halo = round_up(count // 2 + 3, SUBLANES)
    grid = Grid(rows, width, halo)
    order = ring("tm", gray=True)
    sx, sy = ring("sx"), ring("sy")
    middle = rows // 2

    tiles = {}
    onward, backward = c_guess, c_guess
    for s in range(1, count // 2):
        onward, backward = shift(onward, "tm", order, 1), shift(backward, "tm", order, -1)
        tiles[s], tiles[count - s] = onward, backward
    second = shift(onward[:, middle:], "tm", order, 1)
    first = shift(backward[:, :middle], "tm", order, -1)

    fields = (kappa, initial, c_guess[0])
    before = shift(jnp.stack([x[rows - halo :] for x in fields]), "sx", sx, 1)
    after = shift(jnp.stack([x[:halo] for x in fields]), "sx", sx, -1)
    length = round_up(grid.total, LANES)
    packed = (len(fields), halo, length)
    first_cols, last_cols = call(functools.partial(edge_kernel, halo, rows), [packed] * 2)(
        before, after, *[x[:, :LANES] for x in fields], *[x[:, width - LANES :] for x in fields]
    )
    left = shift(last_cols, "sy", sy, 1)
    right = shift(first_cols, "sy", sy, -1)

    strip = jnp.concatenate(
        [jnp.concatenate([before[2], after[2]], axis=0), jnp.concatenate([left[2], right[2]], axis=0)], axis=1
    )
    strips = {s: shift(strip, "tm", order, s) for s in range(1, count)}

    ext, padded = grid.ext, grid.padded
    work = [ext] * 3 + [padded] * 2
    sides = (count // 2, *ext)
    kap, even, tail, low = call(functools.partial(start_kernel, grid), [ext, sides, ext, ext], work)(
        kappa, initial, before, after, left, right
    )
    odd = jnp.zeros(sides, jnp.float32)
    for s in range(1, count // 2):
        aways = sorted({s, count - s})
        pairs = [x for a in aways for x in (tiles[a], strips[a])]
        even, odd, tail = call(
            functools.partial(middle_kernel, grid, order, aways), [sides, sides, ext], work,
            input_output_aliases={1: 0, 2: 1, 3: 2},
        )(kap, even, odd, tail, *pairs)
    c_new, f_new, _, _ = call(
        functools.partial(last_kernel, grid, order), [c_guess.shape] * 2 + [sides, ext], work,
        input_output_aliases={2: 2, 3: 3},
    )(kap, even, odd, tail, low, first, second, strips[count // 2])
    return c_new, f_new


def solution(mesh):
    return jax.shard_map(
        on_device,
        mesh=mesh,
        in_specs=(P("sx", "sy"), P("sx", "sy"), P("tm", "sx", "sy")),
        out_specs=(P("tm", "sx", "sy"), P("tm", "sx", "sy")),
        check_vma=False,
    )
```

```python
import functools
import math
import jax
import jax.numpy as jnp
from jax import lax
from jax.experimental import pallas as pl
from jax.experimental.pallas import tpu as pltpu
from jax.sharding import PartitionSpec as P

LANES = 128
SUBLANES = 8
BLOCK = 16


def round_up(value, step):
    return -(-value // step) * step


def ring(axis, gray=False):
    size = lax.axis_size(axis)
    order = list(range(size))
    if gray and size & (size - 1) == 0:
        order = [i ^ (i >> 1) for i in order]
    return order


def shift(x, axis, order, by):
    size = len(order)
    return lax.ppermute(x, axis, [(order[i], order[(i + by) % size]) for i in range(size)])


def neighbours(axis, to_next, to_previous):
    size, index = lax.axis_size(axis), lax.axis_index(axis)
    even = index % 2 == 0
    got = []
    for start in (0, 1):
        pairs = {i: i for i in range(size)}
        for i in range(start, size - 1, 2):
            pairs[i], pairs[i + 1] = i + 1, i
        send = jnp.where(even == (start == 0), to_next, to_previous)
        got.append(lax.ppermute(send, axis, sorted(pairs.items())))
    from_next = jnp.where(even, got[0], got[1])
    from_previous = jnp.where(even, got[1], got[0])
    return from_previous, from_next


def together(*xs):
    return lax.optimization_barrier(xs)


def call(body, outs, scratch=(), passes=1, semaphores=None, **options):
    cells = sum(math.prod(s) for s in scratch[:1])
    sems = [pltpu.SemaphoreType.DMA(semaphores)] if semaphores else []
    return pl.pallas_call(
        body,
        cost_estimate=pl.CostEstimate(flops=16 * passes * cells, bytes_accessed=24 * passes * cells, transcendentals=0),
        out_shape=[jax.ShapeDtypeStruct(s, jnp.float32) for s in outs],
        scratch_shapes=[pltpu.VMEM(s, jnp.float32) for s in scratch] + sems,
        compiler_params=pltpu.CompilerParams(vmem_limit_bytes=48 * 2**20),
        **options,
    )


def cols_kernel(halo, *refs):
    fields = len(refs) // 2 - 1
    firsts, lasts = refs[:fields], refs[fields : 2 * fields]
    first_out, last_out = refs[2 * fields :]
    for k in range(fields):
        first_out[k] = firsts[k][...].T[:halo]
        last_out[k] = lasts[k][...].T[LANES - halo :]


def rows_kernel(halo, first_rows, last_rows, left, right, first_out, last_out):
    rows, width = left.shape[-1], first_rows.shape[-1]
    iy, last_iy = lax.axis_index("sy"), lax.axis_size("sy") - 1
    gap = jnp.zeros((LANES - 2 * halo, LANES), jnp.float32)
    for k in range(left.shape[0]):
        for given, out, lane, at in ((first_rows, first_out, 0, 0), (last_rows, last_out, rows - LANES, LANES - halo)):
            after, before = right[k, :, lane : lane + LANES], left[k, :, lane : lane + LANES]
            if k == 0:
                after, before = jnp.where(iy == last_iy, 0.0, after), jnp.where(iy == 0, 0.0, before)
            corners = jnp.concatenate([after, gap, before], axis=0).T
            out[k, :, :width] = given[k * halo : (k + 1) * halo]
            out[k, :, width:] = corners[at : at + halo]


class Grid:
    def __init__(self, rows, width, halo, deep):
        self.rows, self.width, self.halo = rows, width, halo
        self.total, self.wide = rows + 2 * halo, width + LANES
        self.deep = deep
        self.high = round_up(2 * deep, SUBLANES)
        self.strip = (2 * self.high, max(width, rows + LANES))
        self.ext = (self.total, self.wide)
        self.padded = (self.total + 2 * SUBLANES, self.wide)

    def fill(self, dst, tile, before, after, left, right):
        rows, halo, total, width = self.rows, self.halo, self.total, self.width
        at = 0
        for part in tile:
            dst[at : at + part.shape[0], 0:width] = part[...]
            at += part.shape[0]
        open_rows = 2 * halo - before.shape[0] - after.shape[0]
        gap = [jnp.zeros((open_rows, self.wide), jnp.float32)] if open_rows else []
        dst[rows:total, :] = jnp.concatenate([after, *gap, before], axis=0)
        gap = jnp.zeros((LANES - left.shape[0] - right.shape[0], rows), jnp.float32)
        dst[0:rows, width:] = jnp.concatenate([right, gap, left], axis=0).T

    def over(self, body, dst=None):
        total = self.total
        for o in range(0, total, BLOCK):
            size = min(BLOCK, total - o)
            value = body(slice(o, o + size))
            if dst is None:
                continue
            dst[o + SUBLANES : o + SUBLANES + size, :] = value
            if o == 0:
                dst[total + SUBLANES :, :] = value[:SUBLANES]
            if o + size == total:
                dst[0:SUBLANES, :] = value[size - SUBLANES :]

    def lap(self, src, at):
        size, wide = at.stop - at.start, self.wide
        around = src[at.start : at.stop + 2 * SUBLANES, :]
        cur = around[SUBLANES : SUBLANES + size]
        up = pltpu.roll(around, 1, 0)[SUBLANES : SUBLANES + size]
        down = pltpu.roll(around, size + 2 * SUBLANES - 1, 0)[SUBLANES : SUBLANES + size]
        return down + up + pltpu.roll(cur, wide - 1, 1) + pltpu.roll(cur, 1, 1) - 4.0 * cur

    def flux(self, kap, src, dst):
        def body(at):
            v = src[at, :]
            return kap[at, :] * v * v

        self.over(body, dst)

    def first_part(self, kap, w, mid, lap_w, fa, fb, out):
        self.flux(kap, w, fa)

        def one(at):
            lw = self.lap(fa, at)
            lap_w[at, :] = lw
            f = w[at, :] + lw
            mid[at, :] = f
            return kap[at, :] * f * f

        self.over(one, fb)

        def two(at):
            v = mid[at, :] + self.lap(fb, at)
            mid[at, :] = v
            out(at, (v - w[at, :]) - 2.0 * lap_w[at, :])
            return kap[at, :] * v * v

        self.over(two, fa)

    def second_part(self, w, mid, lap_w, fa, out):
        def one(at):
            q = w[at, :] + 4.0 * lap_w[at, :]
            out(at, mid[at, :] + 2.0 * self.lap(fa, at) - q)

        self.over(one)


def absorb(grid, kap, point, here, load, even, odd, tail, work):
    wk, mid, lap_w, fa, fb = work
    load(wk)
    step = lax.div(point, 2)

    @pl.when(lax.rem(point, 2) == 1)
    def _():
        def out(at, g):
            odd[step, at, :] = g

        grid.first_part(kap, wk, mid, lap_w, fa, fb, out)

    @pl.when(lax.rem(point, 2) == 0)
    def _():
        def out(at, g):
            tail[at, :] = g

        grid.first_part(kap, wk, mid, lap_w, fa, fb, out)

        @pl.when(point < here)
        def _():
            def out(at, h):
                even[step, at, :] = h

            grid.second_part(wk, mid, lap_w, fa, out)


def start_kernel(grid, kappa, initial, before, after, left, right, kap, even, tail, low, wk, mid, lap_w, fa, fb):
    ix, last_ix = lax.axis_index("sx"), lax.axis_size("sx") - 1
    iy, last_iy = lax.axis_index("sy"), lax.axis_size("sy") - 1
    grid.fill(
        kap, [kappa],
        jnp.where(ix == 0, 0.0, before[0]), jnp.where(ix == last_ix, 0.0, after[0]),
        jnp.where(iy == 0, 0.0, left[0]), jnp.where(iy == last_iy, 0.0, right[0]),
    )
    grid.fill(wk, [initial], before[1], after[1], left[1], right[1])

    def out(at, g):
        x, lx = wk[at, :], lap_w[at, :]
        tail[at, :] = x + 2.0 * lx + g
        low[at, :] = x + lx

    grid.first_part(kap, wk, mid, lap_w, fa, fb, out)

    def out_even(at, h):
        even[0, at, :] = (wk[at, :] + 4.0 * lap_w[at, :]) + h

    grid.second_part(wk, mid, lap_w, fa, out_even)


def arrival(grid, away, tile, strip, kap, order, even, odd, tail, work):
    count = len(order)
    here, point = lax.axis_index("tm"), jnp.int32(count)
    for p in range(count):
        point = jnp.where(here == order[p], order[(p - away) % count] + 1, point)

    def load(wk):
        rows, width, deep, high = grid.rows, grid.width, grid.deep, grid.high
        edge = jnp.concatenate([strip[: 2 * deep, :width], strip[high : high + 2 * deep, rows : rows + LANES]], axis=1)
        cols = strip[high : high + 2 * deep, :rows]
        grid.fill(wk, tile, edge[deep:], edge[:deep], cols[deep:], cols[:deep])

    @pl.when(point <= here)
    def _():
        absorb(grid, kap, point, here, load, even, odd, tail, work)


def middle_kernel(grid, order, aways, kap, even_in, odd_in, tail_in, *refs):
    given, refs = refs[: 2 * len(aways)], refs[2 * len(aways) :]
    even, odd, tail = refs[:3]
    for i, away in enumerate(aways):
        arrival(grid, away, [given[2 * i]], given[2 * i + 1], kap, order, even, odd, tail, refs[3:])


def last_kernel(grid, order, kap, even, odd_in, tail_in, low, first, second, strip, c_out, f_out, odd, tail, *work):
    wk, mid, lap_w, fa, fb = work
    count = len(order)
    here = lax.axis_index("tm")
    rows, width = grid.rows, grid.width
    arrival(grid, count // 2, [first, second], strip, kap, order, even, odd, tail, work)
    state = wk

    def put(dst, at, value):
        stop = min(at.stop, rows)
        if at.start < stop:
            dst[0, at.start : stop, :] = value[: stop - at.start, :width]

    @pl.when(here == 0)
    def _():
        c_out[0] = tail[:rows, :width]
        f_out[0] = low[:rows, :width]

    @pl.when(here == 1)
    def _():
        grid.flux(kap, tail, fa)

        def body(at):
            put(c_out, at, even[0, at, :] + odd[0, at, :])
            put(f_out, at, tail[at, :] + grid.lap(fa, at))

        grid.over(body)

    @pl.when(here >= 2)
    def _():
        def begin(at):
            x = even[0, at, :] + odd[0, at, :]
            state[at, :] = x
            return kap[at, :] * x * x

        grid.over(begin, fb)

        if count > 4:

            def step(j, carry):
                def body(at):
                    x = state[at, :] + 4.0 * grid.lap(fb, at) + (even[j, at, :] + odd[j, at, :])
                    state[at, :] = x
                    return kap[at, :] * x * x

                grid.over(body, fa)
                fb[...] = fa[...]
                return carry

            lax.fori_loop(1, lax.div(here, 2), step, 0)

        @pl.when(lax.rem(here, 2) == 0)
        def _():
            def body(at):
                x, lx = state[at, :], grid.lap(fb, at)
                put(c_out, at, x + 2.0 * lx + tail[at, :])
                put(f_out, at, x + lx)

            grid.over(body)

        @pl.when(lax.rem(here, 2) == 1)
        def _():
            j = lax.div(here, 2)

            def body(at):
                x, lx = state[at, :], grid.lap(fb, at)
                c = x + 2.0 * lx + tail[at, :]
                mid[at, :] = c
                put(c_out, at, x + 4.0 * lx + (even[j, at, :] + odd[j, at, :]))
                return kap[at, :] * c * c

            grid.over(body, fa)

            def last(at):
                put(f_out, at, mid[at, :] + grid.lap(fa, at))

            grid.over(last)


def on_device(initial, kappa, c_guess):
    count = lax.axis_size("tm")
    rows, width = initial.shape
    steps = count // 2
    halo, deep = round_up(steps + 3, SUBLANES), steps + 2
    grid = Grid(rows, width, halo, deep)
    order = ring("tm", gray=True)
    sx = ring("sx")
    middle = rows // 2
    ext, padded = grid.ext, grid.padded
    work = [ext] * 3 + [padded] * 2
    sides = (steps, *ext)

    tiles, strips = {}, {}
    if steps > 1:
        for s in (1, -1):
            tiles[s] = shift(c_guess, "tm", order, s)[0]

    fields = (kappa, initial, c_guess[0])
    packed = (len(fields), halo, rows)
    first_cols, last_cols = call(functools.partial(cols_kernel, halo), [packed] * 2)(
        *[x[:, :LANES] for x in fields], *[x[:, width - LANES :] for x in fields]
    )
    left, right = neighbours("sy", last_cols, first_cols)
    packed = (len(fields), halo, grid.wide)
    first_rows, last_rows = call(functools.partial(rows_kernel, halo), [packed] * 2)(
        jnp.concatenate([x[:halo] for x in fields], axis=0),
        jnp.concatenate([x[rows - halo :] for x in fields], axis=0),
        left, right,
    )
    before, after = shift(last_rows, "sx", sx, 1), shift(first_rows, "sx", sx, -1)

    def padded_to(x, shape):
        return jnp.pad(x, [(0, n - m) for m, n in zip(x.shape, shape)])

    part = (grid.high, grid.strip[1])
    edge = jnp.concatenate([after[2, :deep], before[2, halo - deep :]], axis=0)
    cols = jnp.concatenate([right[2, :deep], left[2, halo - deep :]], axis=0)
    strip = jnp.concatenate(
        [padded_to(edge[:, :width], part), padded_to(jnp.concatenate([cols, edge[:, width:]], axis=1), part)], axis=0
    )
    if steps > 1:
        for s in (1, -1):
            strips[s] = shift(strip, "tm", order, s)

    before, strip = together(before, strip)
    kap, even, tail, low = call(functools.partial(start_kernel, grid), [ext, sides, ext, ext], work, 4)(
        kappa, initial, before, after, left, right
    )
    odd = jnp.zeros(sides, jnp.float32)

    if steps == 1:
        tiles, strips = {1: c_guess[0], -1: c_guess[0]}, {1: strip}
    for s in range(1, steps):
        given = [x for way in (1, -1) for x in (tiles[way], strips[way])]
        strips = {way: shift(x, "tm", order, way) for way, x in strips.items() if s + 1 < steps or way == 1}
        if s + 1 < steps:
            tiles = {way: shift(x, "tm", order, way) for way, x in tiles.items()}
        else:
            second = shift(tiles[1][middle:], "tm", order, 1)
            first = shift(tiles[-1][:middle], "tm", order, -1)
        even, odd, tail = call(
            functools.partial(middle_kernel, grid, order, (s, count - s)), [sides, sides, ext], work, 1000,
            input_output_aliases={1: 0, 2: 1, 3: 2},
        )(kap, even, odd, tail, *given)
    if steps == 1:
        second, first = shift(tiles[1][middle:], "tm", order, 1), shift(tiles[-1][:middle], "tm", order, -1)
        strips = {1: shift(strip, "tm", order, 1)}
    c_new, f_new, _, _ = call(
        functools.partial(last_kernel, grid, order), [c_guess.shape] * 2 + [sides, ext], work, 8,
        input_output_aliases={2: 2, 3: 3},
    )(kap, even, odd, tail, low, first, second, strips[1])
    return c_new, f_new


def solution(mesh):
    return jax.shard_map(
        on_device,
        mesh=mesh,
        in_specs=(P("sx", "sy"), P("sx", "sy"), P("tm", "sx", "sy")),
        out_specs=(P("tm", "sx", "sy"), P("tm", "sx", "sy")),
        check_vma=False,
    )
```

```python
import functools
import math
import jax
import jax.numpy as jnp
from jax import lax
from jax.experimental import pallas as pl
from jax.experimental.pallas import tpu as pltpu
from jax.sharding import PartitionSpec as P

LANES = 128
SUBLANES = 8
BLOCK = 16
SHARE = 7 / 16
MIDDLE = 405


def round_up(value, step):
    return -(-value // step) * step


def swap(x, axis, bits):
    return lax.ppermute(x, axis, [(i, i ^ bits) for i in range(lax.axis_size(axis))])


def neighbours(axis, to_next, to_previous):
    size, index = lax.axis_size(axis), lax.axis_index(axis)
    even = index % 2 == 0
    got = []
    for start in (0, 1):
        pairs = {i: i for i in range(size)}
        for i in range(start, size - 1, 2):
            pairs[i], pairs[i + 1] = i + 1, i
        send = jnp.where(even == (start == 0), to_next, to_previous)
        got.append(lax.ppermute(send, axis, sorted(pairs.items())) if size > start + 1 else send)
    from_next = jnp.where(even, got[0], got[1])
    from_previous = jnp.where(even, got[1], got[0])
    return from_previous, from_next


def together(*xs):
    return lax.optimization_barrier(xs)


def call(body, outs, scratch=(), passes=1, semaphores=None, **options):
    cells = sum(math.prod(s) for s in scratch[:1])
    sems = [pltpu.SemaphoreType.DMA(semaphores)] if semaphores else []
    return pl.pallas_call(
        body,
        cost_estimate=pl.CostEstimate(flops=16 * passes * cells, bytes_accessed=24 * passes * cells, transcendentals=0),
        out_shape=[jax.ShapeDtypeStruct(s, jnp.float32) for s in outs],
        scratch_shapes=[pltpu.VMEM(s, jnp.float32) for s in scratch] + sems,
        compiler_params=pltpu.CompilerParams(vmem_limit_bytes=48 * 2**20),
        **options,
    )


def cols_kernel(halo, *refs):
    fields = len(refs) // 2 - 1
    firsts, lasts = refs[:fields], refs[fields : 2 * fields]
    first_out, last_out = refs[2 * fields :]
    for k in range(fields):
        first_out[k] = firsts[k][...].T[:halo]
        last_out[k] = lasts[k][...].T[LANES - halo :]


def rows_kernel(halo, first_rows, last_rows, left, right, first_out, last_out):
    rows, width = left.shape[-1], first_rows.shape[-1]
    iy, last_iy = lax.axis_index("sy"), lax.axis_size("sy") - 1
    gap = jnp.zeros((LANES - 2 * halo, LANES), jnp.float32)
    for k in range(left.shape[0]):
        for given, out, lane, at in ((first_rows, first_out, 0, 0), (last_rows, last_out, rows - LANES, LANES - halo)):
            after, before = right[k, :, lane : lane + LANES], left[k, :, lane : lane + LANES]
            if k == 0:
                after, before = jnp.where(iy == last_iy, 0.0, after), jnp.where(iy == 0, 0.0, before)
            corners = jnp.concatenate([after, gap, before], axis=0).T
            out[k, :, :width] = given[k * halo : (k + 1) * halo]
            out[k, :, width:] = corners[at : at + halo]


class Grid:
    def __init__(self, rows, width, halo, deep):
        self.rows, self.width, self.halo = rows, width, halo
        self.total, self.wide = rows + 2 * halo, width + LANES
        self.deep = deep
        self.high = round_up(2 * deep, SUBLANES)
        self.strip = (2 * self.high, max(width, rows + LANES))
        self.ext = (self.total, self.wide)
        self.padded = (self.total + 2 * SUBLANES, self.wide)

    def fill(self, dst, tile, before, after, left, right, kap=None, flux=None):
        rows, halo, total, width = self.rows, self.halo, self.total, self.width
        open_rows = 2 * halo - before.shape[0] - after.shape[0]
        gap = [jnp.zeros((open_rows, self.wide), jnp.float32)] if open_rows else []
        dst[rows:total, :] = jnp.concatenate([after, *gap, before], axis=0)
        gap = jnp.zeros((LANES - left.shape[0] - right.shape[0], rows), jnp.float32)
        dst[0:rows, width:] = jnp.concatenate([right, gap, left], axis=0).T
        parts, start = [], 0
        for part in tile:
            parts.append((start, start + part.shape[0], part))
            start += part.shape[0]

        def body(at):
            for first, stop, part in parts:
                lo, hi = max(at.start, first), min(at.stop, stop)
                if lo < hi:
                    dst[lo:hi, 0:width] = part[lo - first : hi - first, :]
            if flux is not None:
                v = dst[at, :]
                return kap[at, :] * v * v

        self.over(body, flux)

    def over(self, body, dst=None):
        total = self.total
        for o in range(0, total, BLOCK):
            size = min(BLOCK, total - o)
            value = body(slice(o, o + size))
            if dst is None:
                continue
            dst[o + SUBLANES : o + SUBLANES + size, :] = value
            if o == 0:
                dst[total + SUBLANES :, :] = value[:SUBLANES]
            if o + size == total:
                dst[0:SUBLANES, :] = value[size - SUBLANES :]

    def lap(self, src, at):
        size, wide = at.stop - at.start, self.wide
        around = src[at.start : at.stop + 2 * SUBLANES, :]
        cur = around[SUBLANES : SUBLANES + size]
        up = pltpu.roll(around, 1, 0)[SUBLANES : SUBLANES + size]
        down = pltpu.roll(around, size + 2 * SUBLANES - 1, 0)[SUBLANES : SUBLANES + size]
        return down + up + pltpu.roll(cur, wide - 1, 1) + pltpu.roll(cur, 1, 1) - 4.0 * cur

    def flux(self, kap, src, dst):
        def body(at):
            v = src[at, :]
            return kap[at, :] * v * v

        self.over(body, dst)

    def first_part(self, kap, w, mid, lap_w, fa, fb, out, more=True, fc=None):

        def one(at):
            lw = self.lap(fa, at)
            lap_w[at, :] = lw
            f = w[at, :] + lw
            mid[at, :] = f
            return kap[at, :] * f * f

        self.over(one, fb)

        def two(at):
            v = mid[at, :] + self.lap(fb, at)
            if more:
                mid[at, :] = v
            value = out(at, (v - w[at, :]) - 2.0 * lap_w[at, :])
            return kap[at, :] * v * v if more else value

        self.over(two, fa if more else fc)

    def second_part(self, w, mid, lap_w, fa, out):
        def one(at):
            q = w[at, :] + 4.0 * lap_w[at, :]
            out(at, mid[at, :] + 2.0 * self.lap(fa, at) - q)

        self.over(one)


def absorb(grid, kap, point, here, load, even, odd, tail, work, own_only=False):
    wk, mid, lap_w, fa, fb = work
    load(wk, fa)
    step = lax.div(point, 2)

    @pl.when(lax.rem(point, 2) == 1)
    def _():
        def out(at, g):
            odd[step, at, :] = g

        grid.first_part(kap, wk, mid, lap_w, fa, fb, out, False)

    @pl.when(lax.rem(point, 2) == 0)
    def _():
        def out(at, g):
            tail[at, :] = g

        grid.first_part(kap, wk, mid, lap_w, fa, fb, out, not own_only)
        if own_only:
            return

        @pl.when(point < here)
        def _():
            def out(at, h):
                even[step, at, :] = h

            grid.second_part(wk, mid, lap_w, fa, out)


def start_kernel(grid, kappa, initial, before, after, left, right, kap, even, tail, low, wk, mid, lap_w, fa, fb):
    ix, last_ix = lax.axis_index("sx"), lax.axis_size("sx") - 1
    iy, last_iy = lax.axis_index("sy"), lax.axis_size("sy") - 1
    grid.fill(
        kap, [kappa],
        jnp.where(ix == 0, 0.0, before[0]), jnp.where(ix == last_ix, 0.0, after[0]),
        jnp.where(iy == 0, 0.0, left[0]), jnp.where(iy == last_iy, 0.0, right[0]),
    )
    grid.fill(wk, [initial], before[1], after[1], left[1], right[1], kap, fa)

    def out(at, g):
        x, lx = wk[at, :], lap_w[at, :]
        tail[at, :] = x + 2.0 * lx + g
        low[at, :] = x + lx

    grid.first_part(kap, wk, mid, lap_w, fa, fb, out)

    def out_even(at, h):
        even[0, at, :] = (wk[at, :] + 4.0 * lap_w[at, :]) + h

    grid.second_part(wk, mid, lap_w, fa, out_even)


def loader(grid, kap, tile, strip):
    def load(wk, flux):
        rows, width, deep, high = grid.rows, grid.width, grid.deep, grid.high
        edge = jnp.concatenate([strip[: 2 * deep, :width], strip[high : high + 2 * deep, rows : rows + LANES]], axis=1)
        cols = strip[high : high + 2 * deep, :rows]
        grid.fill(wk, tile, edge[deep:], edge[:deep], cols[deep:], cols[:deep], kap, flux)

    return load


def middle_kernel(grid, bits, kap, even_in, odd_in, tail_in, tile, strip, even, odd, tail, *work):
    here = lax.axis_index("tm")
    point = (here ^ bits) + 1

    @pl.when(point <= here)
    def _():
        absorb(grid, kap, point, here, loader(grid, kap, [tile], strip), even, odd, tail, work)


def last_kernel(grid, count, kap, even, odd_in, tail_in, low, first, second, strip, c_out, f_out, odd, tail, *work):
    wk, mid, lap_w, fa, fb, fc, c_rows, f_rows, sems = work
    here = lax.axis_index("tm")
    point = (here ^ (count - 1)) + 1
    rows, width = grid.rows, grid.width
    load = loader(grid, kap, [first, second], strip)
    state = wk
    chunk = round_up(-(-rows // sems.shape[1]), BLOCK)

    def sent(which, i):
        src, dst = ((c_rows, c_out), (f_rows, f_out))[which]
        part = slice(i * chunk, min((i + 1) * chunk, rows))
        return pltpu.make_async_copy(src.at[part], dst.at[0, part], sems.at[which, i])

    def put(which, at, value):
        stop = min(at.stop, rows)
        if at.start < stop:
            (c_rows, f_rows)[which][at.start : stop, :] = value[: stop - at.start, :width]
            if stop % chunk == 0 or stop == rows:
                sent(which, (stop - 1) // chunk).start()

    @pl.when(here == 0)
    def _():
        def body(at):
            put(0, at, tail[at, :])
            put(1, at, low[at, :])

        grid.over(body)

    @pl.when(here == 1)
    def _():
        def body(at):
            c = tail[at, :]
            put(0, at, even[0, at, :] + odd[0, at, :])
            return kap[at, :] * c * c

        grid.over(body, fa)

        def last(at):
            put(1, at, tail[at, :] + grid.lap(fa, at))

        grid.over(last)

    @pl.when(here >= 2)
    def _():
        @pl.when(point == 1)
        def _():
            load(wk, fa)

            def out(at, g):
                x = even[0, at, :] + g
                state[at, :] = x
                return kap[at, :] * x * x

            grid.first_part(kap, wk, mid, lap_w, fa, fb, out, False, fc)

        @pl.when(point != 1)
        def _():
            @pl.when(point <= here)
            def _():
                absorb(grid, kap, point, here, load, even, odd, tail, work[:5], count == 4)

            def begin(at):
                x = even[0, at, :] + odd[0, at, :]
                state[at, :] = x
                return kap[at, :] * x * x

            grid.over(begin, fc)

        if count > 4:

            def step(j, carry):
                def body(at):
                    x = state[at, :] + 4.0 * grid.lap(fc, at) + (even[j, at, :] + odd[j, at, :])
                    state[at, :] = x
                    return kap[at, :] * x * x

                grid.over(body, fa)
                fc[...] = fa[...]
                return carry

            lax.fori_loop(1, lax.div(here, 2), step, 0)

        @pl.when(lax.rem(here, 2) == 0)
        def _():
            def body(at):
                x, lx = state[at, :], grid.lap(fc, at)
                put(0, at, x + 2.0 * lx + tail[at, :])
                put(1, at, x + lx)

            grid.over(body)

        @pl.when(lax.rem(here, 2) == 1)
        def _():
            j = lax.div(here, 2)

            def body(at):
                x, lx = state[at, :], grid.lap(fc, at)
                c = x + 2.0 * lx + tail[at, :]
                mid[at, :] = c
                put(0, at, x + 4.0 * lx + (even[j, at, :] + odd[j, at, :]))
                return kap[at, :] * c * c

            grid.over(body, fa)

            def last(at):
                put(1, at, mid[at, :] + grid.lap(fa, at))

            grid.over(last)

    for which in (0, 1):
        for i in range(-(-rows // chunk)):
            sent(which, i).wait()


def on_device(initial, kappa, c_guess):
    count = lax.axis_size("tm")
    rows, width = initial.shape
    steps = count // 2
    halo, deep = round_up(steps + 3, SUBLANES), steps + 2
    grid = Grid(rows, width, halo, deep)
    share = round_up(int(rows * SHARE), BLOCK)
    ext, padded = grid.ext, grid.padded
    work = [ext] * 3 + [padded] * 2
    sides = (steps, *ext)

    tiles, strips = {0: c_guess[0]}, {}
    singles = [1 << i for i in range((count - 1).bit_length())]
    several = sorted((d for d in range(1, count - 1) if d not in singles), key=lambda d: d.bit_count())
    for bit in singles:
        if bit < count - 1:
            tiles[bit] = swap(c_guess, "tm", bit)[0]

    fields = (kappa, initial, c_guess[0])
    packed = (len(fields), halo, rows)
    first_cols, last_cols = call(functools.partial(cols_kernel, halo), [packed] * 2)(
        *[x[:, :LANES] for x in fields], *[x[:, width - LANES :] for x in fields]
    )
    left, right = neighbours("sy", last_cols, first_cols)
    packed = (len(fields), halo, grid.wide)
    first_rows, last_rows = call(functools.partial(rows_kernel, halo), [packed] * 2)(
        jnp.concatenate([x[:halo] for x in fields], axis=0),
        jnp.concatenate([x[rows - halo :] for x in fields], axis=0),
        left, right,
    )
    before, after = neighbours("sx", last_rows, first_rows)

    def padded_to(x, shape):
        return jnp.pad(x, [(0, n - m) for m, n in zip(x.shape, shape)])

    part = (grid.high, grid.strip[1])
    edge = jnp.concatenate([after[2, :deep], before[2, halo - deep :]], axis=0)
    cols = jnp.concatenate([right[2, :deep], left[2, halo - deep :]], axis=0)
    strip = jnp.concatenate(
        [padded_to(edge[:, :width], part), padded_to(jnp.concatenate([cols, edge[:, width:]], axis=1), part)], axis=0
    )
    strips[0] = strip
    for bit in singles:
        if bit < count - 1:
            strips[bit] = swap(strip, "tm", bit)

    before, strip = together(before, strip)
    kap, even, tail, low = call(functools.partial(start_kernel, grid), [ext, sides, ext, ext], work, 4)(
        kappa, initial, before, after, left, right
    )
    odd = jnp.zeros(sides, jnp.float32)

    for d in several:
        bit = d & -d
        tiles[d], strips[d] = swap(tiles[d ^ bit], "tm", bit), swap(strips[d ^ bit], "tm", bit)
    near, far, last = singles[0], singles[-1], count - 1
    first, second = swap(tiles[last ^ near][:share], "tm", near), swap(tiles[last ^ far][share:], "tm", far)
    strips[last] = swap(strips[last ^ near], "tm", near)
    for d in (*singles, *several):
        if d != last:
            even, odd, tail = call(
                functools.partial(middle_kernel, grid, d), [sides, sides, ext], work, MIDDLE,
                input_output_aliases={1: 0, 2: 1, 3: 2},
            )(kap, even, odd, tail, tiles[d], strips[d])
    c_new, f_new, _, _ = call(
        functools.partial(last_kernel, grid, count), [c_guess.shape] * 2 + [sides, ext],
        work + [padded] + [(rows, width)] * 2, 8, semaphores=(2, 4), input_output_aliases={2: 2, 3: 3},
        out_specs=[pl.BlockSpec(memory_space=space) for space in (pl.ANY, pl.ANY, pltpu.VMEM, pltpu.VMEM)],
    )(kap, even, odd, tail, low, first, second, strips[last])
    return c_new, f_new


def solution(mesh):
    return jax.shard_map(
        on_device,
        mesh=mesh,
        in_specs=(P("sx", "sy"), P("sx", "sy"), P("tm", "sx", "sy")),
        out_specs=(P("tm", "sx", "sy"), P("tm", "sx", "sy")),
        check_vma=False,
    )
```

```python
import functools
import math
import jax
import jax.numpy as jnp
from jax import lax
from jax.experimental import pallas as pl
from jax.experimental.pallas import tpu as pltpu
from jax.sharding import PartitionSpec as P

LANES = 128
SUBLANES = 8
BLOCK = 16
SHARE = 7 / 16
MIDDLE = 405


def round_up(value, step):
    return -(-value // step) * step


def swap(x, axis, bits):
    return lax.ppermute(x, axis, [(i, i ^ bits) for i in range(lax.axis_size(axis))])


def neighbours(axis, to_next, to_previous):
    size, index = lax.axis_size(axis), lax.axis_index(axis)
    even = index % 2 == 0
    got = []
    for start in (0, 1):
        pairs = {i: i for i in range(size)}
        for i in range(start, size - 1, 2):
            pairs[i], pairs[i + 1] = i + 1, i
        send = jnp.where(even == (start == 0), to_next, to_previous)
        got.append(lax.ppermute(send, axis, sorted(pairs.items())) if size > start + 1 else send)
    from_next = jnp.where(even, got[0], got[1])
    from_previous = jnp.where(even, got[1], got[0])
    return from_previous, from_next


def together(*xs):
    return lax.optimization_barrier(xs)


def call(body, outs, scratch=(), passes=1, semaphores=None, **options):
    cells = sum(math.prod(s) for s in scratch[:1])
    sems = [pltpu.SemaphoreType.DMA(semaphores)] if semaphores else []
    return pl.pallas_call(
        body,
        cost_estimate=pl.CostEstimate(flops=16 * passes * cells, bytes_accessed=24 * passes * cells, transcendentals=0),
        out_shape=[jax.ShapeDtypeStruct(s, jnp.float32) for s in outs],
        scratch_shapes=[pltpu.VMEM(s, jnp.float32) for s in scratch] + sems,
        compiler_params=pltpu.CompilerParams(vmem_limit_bytes=48 * 2**20),
        **options,
    )


def cols_kernel(halo, *refs):
    *fields, first_out, last_out = refs
    for k, field in enumerate(fields):
        width = field.shape[1]
        first_out[k] = field[:, :LANES].T[:halo]
        last_out[k] = field[:, width - LANES :].T[LANES - halo :]


def rows_kernel(halo, first_rows, last_rows, left, right, first_out, last_out):
    rows, width = left.shape[-1], first_rows.shape[-1]
    iy, last_iy = lax.axis_index("sy"), lax.axis_size("sy") - 1
    gap = jnp.zeros((LANES - 2 * halo, LANES), jnp.float32)
    for k in range(left.shape[0]):
        for given, out, lane, at in ((first_rows, first_out, 0, 0), (last_rows, last_out, rows - LANES, LANES - halo)):
            after, before = right[k, :, lane : lane + LANES], left[k, :, lane : lane + LANES]
            if k == 0:
                after, before = jnp.where(iy == last_iy, 0.0, after), jnp.where(iy == 0, 0.0, before)
            corners = jnp.concatenate([after, gap, before], axis=0).T
            out[k, :, :width] = given[k * halo : (k + 1) * halo]
            out[k, :, width:] = corners[at : at + halo]


class Grid:
    def __init__(self, rows, width, halo, deep):
        self.rows, self.width, self.halo = rows, width, halo
        self.total, self.wide = rows + 2 * halo, width + LANES
        self.deep = deep
        self.high = round_up(2 * deep, SUBLANES)
        self.strip = (2 * self.high, max(width, rows + LANES))
        self.ext = (self.total, self.wide)
        self.padded = (self.total + 2 * SUBLANES, self.wide)

    def fill(self, dst, tile, before, after, left, right, kap=None, flux=None):
        rows, halo, total, width = self.rows, self.halo, self.total, self.width
        open_rows = 2 * halo - before.shape[0] - after.shape[0]
        gap = [jnp.zeros((open_rows, self.wide), jnp.float32)] if open_rows else []
        dst[rows:total, :] = jnp.concatenate([after, *gap, before], axis=0)
        gap = jnp.zeros((LANES - left.shape[0] - right.shape[0], rows), jnp.float32)
        dst[0:rows, width:] = jnp.concatenate([right, gap, left], axis=0).T
        parts, start = [], 0
        for part in tile:
            parts.append((start, start + part.shape[0], part))
            start += part.shape[0]

        def body(at):
            for first, stop, part in parts:
                lo, hi = max(at.start, first), min(at.stop, stop)
                if lo < hi:
                    dst[lo:hi, 0:width] = part[lo - first : hi - first, :]
            if flux is not None:
                v = dst[at, :]
                return kap[at, :] * v * v

        self.over(body, flux)

    def over(self, body, dst=None):
        total = self.total
        for o in range(0, total, BLOCK):
            size = min(BLOCK, total - o)
            value = body(slice(o, o + size))
            if dst is None:
                continue
            dst[o + SUBLANES : o + SUBLANES + size, :] = value
            if o == 0:
                dst[total + SUBLANES :, :] = value[:SUBLANES]
            if o + size == total:
                dst[0:SUBLANES, :] = value[size - SUBLANES :]

    def lap(self, src, at):
        size, wide = at.stop - at.start, self.wide
        around = src[at.start : at.stop + 2 * SUBLANES, :]
        cur = around[SUBLANES : SUBLANES + size]
        up = pltpu.roll(around, 1, 0)[SUBLANES : SUBLANES + size]
        down = pltpu.roll(around, size + 2 * SUBLANES - 1, 0)[SUBLANES : SUBLANES + size]
        return down + up + pltpu.roll(cur, wide - 1, 1) + pltpu.roll(cur, 1, 1) - 4.0 * cur

    def flux(self, kap, src, dst):
        def body(at):
            v = src[at, :]
            return kap[at, :] * v * v

        self.over(body, dst)

    def first_part(self, kap, w, mid, lap_w, fa, fb, out, more=True, fc=None):

        def one(at):
            lw = self.lap(fa, at)
            lap_w[at, :] = lw
            f = w[at, :] + lw
            mid[at, :] = f
            return kap[at, :] * f * f

        self.over(one, fb)

        def two(at):
            v = mid[at, :] + self.lap(fb, at)
            if more:
                mid[at, :] = v
            value = out(at, (v - w[at, :]) - 2.0 * lap_w[at, :])
            return kap[at, :] * v * v if more else value

        self.over(two, fa if more else fc)

    def second_part(self, w, mid, lap_w, fa, out):
        def one(at):
            q = w[at, :] + 4.0 * lap_w[at, :]
            out(at, mid[at, :] + 2.0 * self.lap(fa, at) - q)

        self.over(one)


def absorb(grid, kap, point, here, load, even, odd, tail, work, own_only=False):
    wk, mid, lap_w, fa, fb = work
    load(wk, fa)
    step = lax.div(point, 2)

    @pl.when(lax.rem(point, 2) == 1)
    def _():
        def out(at, g):
            odd[step, at, :] = g

        grid.first_part(kap, wk, mid, lap_w, fa, fb, out, False)

    @pl.when(lax.rem(point, 2) == 0)
    def _():
        def out(at, g):
            tail[at, :] = g

        grid.first_part(kap, wk, mid, lap_w, fa, fb, out, not own_only)
        if own_only:
            return

        @pl.when(point < here)
        def _():
            def out(at, h):
                even[step, at, :] = h

            grid.second_part(wk, mid, lap_w, fa, out)


def start_kernel(grid, kappa, initial, before, after, left, right, kap, even, tail, low, wk, mid, lap_w, fa, fb):
    ix, last_ix = lax.axis_index("sx"), lax.axis_size("sx") - 1
    iy, last_iy = lax.axis_index("sy"), lax.axis_size("sy") - 1
    grid.fill(
        kap, [kappa],
        jnp.where(ix == 0, 0.0, before[0]), jnp.where(ix == last_ix, 0.0, after[0]),
        jnp.where(iy == 0, 0.0, left[0]), jnp.where(iy == last_iy, 0.0, right[0]),
    )
    grid.fill(wk, [initial], before[1], after[1], left[1], right[1], kap, fa)

    def out(at, g):
        x, lx = wk[at, :], lap_w[at, :]
        tail[at, :] = x + 2.0 * lx + g
        low[at, :] = x + lx

    grid.first_part(kap, wk, mid, lap_w, fa, fb, out)

    def out_even(at, h):
        even[0, at, :] = (wk[at, :] + 4.0 * lap_w[at, :]) + h

    grid.second_part(wk, mid, lap_w, fa, out_even)


def loader(grid, kap, tile, strip):
    def load(wk, flux):
        rows, width, deep, high = grid.rows, grid.width, grid.deep, grid.high
        edge = jnp.concatenate([strip[: 2 * deep, :width], strip[high : high + 2 * deep, rows : rows + LANES]], axis=1)
        cols = strip[high : high + 2 * deep, :rows]
        grid.fill(wk, tile, edge[deep:], edge[:deep], cols[deep:], cols[:deep], kap, flux)

    return load


def middle_kernel(grid, bits, kap, even_in, odd_in, tail_in, tile, strip, even, odd, tail, *work):
    here = lax.axis_index("tm")
    point = (here ^ bits) + 1

    @pl.when(point <= here)
    def _():
        absorb(grid, kap, point, here, loader(grid, kap, [tile], strip), even, odd, tail, work)


def last_kernel(grid, count, kap, even, odd_in, tail_in, low, first, second, strip, c_out, f_out, odd, tail, *work):
    wk, mid, lap_w, fa, fb, fc, c_rows, f_rows, sems = work
    here = lax.axis_index("tm")
    point = (here ^ (count - 1)) + 1
    rows, width = grid.rows, grid.width
    load = loader(grid, kap, [first, second], strip)
    state = wk
    chunk = round_up(-(-rows // sems.shape[1]), BLOCK)

    def sent(which, i):
        src, dst = ((c_rows, c_out), (f_rows, f_out))[which]
        part = slice(i * chunk, min((i + 1) * chunk, rows))
        return pltpu.make_async_copy(src.at[part], dst.at[0, part], sems.at[which, i])

    def put(which, at, value):
        stop = min(at.stop, rows)
        if at.start < stop:
            (c_rows, f_rows)[which][at.start : stop, :] = value[: stop - at.start, :width]
            if stop % chunk == 0 or stop == rows:
                sent(which, (stop - 1) // chunk).start()

    @pl.when(here == 0)
    def _():
        def body(at):
            put(0, at, tail[at, :])
            put(1, at, low[at, :])

        grid.over(body)

    @pl.when(here == 1)
    def _():
        def body(at):
            c = tail[at, :]
            put(0, at, even[0, at, :] + odd[0, at, :])
            return kap[at, :] * c * c

        grid.over(body, fa)

        def last(at):
            put(1, at, tail[at, :] + grid.lap(fa, at))

        grid.over(last)

    @pl.when(here >= 2)
    def _():
        @pl.when(point == 1)
        def _():
            load(wk, fa)

            def out(at, g):
                x = even[0, at, :] + g
                state[at, :] = x
                return kap[at, :] * x * x

            grid.first_part(kap, wk, mid, lap_w, fa, fb, out, False, fc)

        @pl.when(point != 1)
        def _():
            @pl.when(point <= here)
            def _():
                absorb(grid, kap, point, here, load, even, odd, tail, work[:5], count == 4)

            def begin(at):
                x = even[0, at, :] + odd[0, at, :]
                state[at, :] = x
                return kap[at, :] * x * x

            grid.over(begin, fc)

        if count > 4:

            def step(j, carry):
                def body(at):
                    x = state[at, :] + 4.0 * grid.lap(fc, at) + (even[j, at, :] + odd[j, at, :])
                    state[at, :] = x
                    return kap[at, :] * x * x

                grid.over(body, fa)
                fc[...] = fa[...]
                return carry

            lax.fori_loop(1, lax.div(here, 2), step, 0)

        @pl.when(lax.rem(here, 2) == 0)
        def _():
            def body(at):
                x, lx = state[at, :], grid.lap(fc, at)
                put(0, at, x + 2.0 * lx + tail[at, :])
                put(1, at, x + lx)

            grid.over(body)

        @pl.when(lax.rem(here, 2) == 1)
        def _():
            j = lax.div(here, 2)

            def body(at):
                x, lx = state[at, :], grid.lap(fc, at)
                c = x + 2.0 * lx + tail[at, :]
                mid[at, :] = c
                put(0, at, x + 4.0 * lx + (even[j, at, :] + odd[j, at, :]))
                return kap[at, :] * c * c

            grid.over(body, fa)

            def last(at):
                put(1, at, mid[at, :] + grid.lap(fa, at))

            grid.over(last)

    for which in (0, 1):
        for i in range(-(-rows // chunk)):
            sent(which, i).wait()


def on_device(initial, kappa, c_guess):
    count = lax.axis_size("tm")
    rows, width = initial.shape
    steps = count // 2
    halo, deep = round_up(steps + 3, SUBLANES), steps + 2
    grid = Grid(rows, width, halo, deep)
    share = round_up(int(rows * SHARE), BLOCK)
    ext, padded = grid.ext, grid.padded
    work = [ext] * 3 + [padded] * 2
    sides = (steps, *ext)

    tiles, strips = {0: c_guess[0]}, {}
    singles = [1 << i for i in range((count - 1).bit_length())]
    several = sorted((d for d in range(1, count - 1) if d not in singles), key=lambda d: d.bit_count())
    for bit in singles:
        if bit < count - 1:
            tiles[bit] = swap(c_guess, "tm", bit)[0]

    fields = (kappa, initial, c_guess[0])
    packed = (len(fields), halo, rows)
    first_cols, last_cols = call(functools.partial(cols_kernel, halo), [packed] * 2)(
        kappa, initial, jnp.concatenate([c_guess[0, :, :LANES], c_guess[0, :, width - LANES :]], axis=1)
    )
    left, right = neighbours("sy", last_cols, first_cols)
    packed = (len(fields), halo, grid.wide)
    first_rows, last_rows = call(functools.partial(rows_kernel, halo), [packed] * 2)(
        jnp.concatenate([x[:halo] for x in fields], axis=0),
        jnp.concatenate([x[rows - halo :] for x in fields], axis=0),
        left, right,
    )
    before, after = neighbours("sx", last_rows, first_rows)

    def padded_to(x, shape):
        return jnp.pad(x, [(0, n - m) for m, n in zip(x.shape, shape)])

    part = (grid.high, grid.strip[1])
    edge = jnp.concatenate([after[2, :deep], before[2, halo - deep :]], axis=0)
    cols = jnp.concatenate([right[2, :deep], left[2, halo - deep :]], axis=0)
    strip = jnp.concatenate(
        [padded_to(edge[:, :width], part), padded_to(jnp.concatenate([cols, edge[:, width:]], axis=1), part)], axis=0
    )
    strips[0] = strip
    for bit in singles:
        if bit < count - 1:
            strips[bit] = swap(strip, "tm", bit)

    before, strip = together(before, strip)
    kap, even, tail, low = call(functools.partial(start_kernel, grid), [ext, sides, ext, ext], work, 4)(
        kappa, initial, before, after, left, right
    )
    odd = jnp.zeros(sides, jnp.float32)

    for d in several:
        bit = d & -d
        tiles[d], strips[d] = swap(tiles[d ^ bit], "tm", bit), swap(strips[d ^ bit], "tm", bit)
    near, far, last = singles[0], singles[-1], count - 1
    first, second = swap(tiles[last ^ near][:share], "tm", near), swap(tiles[last ^ far][share:], "tm", far)
    strips[last] = swap(strips[last ^ near], "tm", near)
    for d in (*singles, *several):
        if d != last:
            even, odd, tail = call(
                functools.partial(middle_kernel, grid, d), [sides, sides, ext], work, MIDDLE,
                input_output_aliases={1: 0, 2: 1, 3: 2},
            )(kap, even, odd, tail, tiles[d], strips[d])
    c_new, f_new, _, _ = call(
        functools.partial(last_kernel, grid, count), [c_guess.shape] * 2 + [sides, ext],
        work + [padded] + [(rows, width)] * 2, 8, semaphores=(2, 4), input_output_aliases={2: 2, 3: 3},
        out_specs=[pl.BlockSpec(memory_space=space) for space in (pl.ANY, pl.ANY, pltpu.VMEM, pltpu.VMEM)],
    )(kap, even, odd, tail, low, first, second, strips[last])
    return c_new, f_new


def solution(mesh):
    return jax.shard_map(
        on_device,
        mesh=mesh,
        in_specs=(P("sx", "sy"), P("sx", "sy"), P("tm", "sx", "sy")),
        out_specs=(P("tm", "sx", "sy"), P("tm", "sx", "sy")),
        check_vma=False,
    )
```

```python
import functools
import math
import jax
import jax.numpy as jnp
from jax import lax
from jax.experimental import pallas as pl
from jax.experimental.pallas import tpu as pltpu
from jax.sharding import PartitionSpec as P

LANES = 128
SUBLANES = 8
BLOCK = 16
CHUNKS = 8
SHARE = 15 / 32
MIDDLE = 430


def round_up(value, step):
    return -(-value // step) * step


def swap(x, axis, bits):
    return lax.ppermute(x, axis, [(i, i ^ bits) for i in range(lax.axis_size(axis))])


def neighbours(axis, to_next, to_previous):
    size, index = lax.axis_size(axis), lax.axis_index(axis)
    even = index % 2 == 0
    got = []
    for start in (0, 1):
        pairs = {i: i for i in range(size)}
        for i in range(start, size - 1, 2):
            pairs[i], pairs[i + 1] = i + 1, i
        send = jnp.where(even == (start == 0), to_next, to_previous)
        got.append(lax.ppermute(send, axis, sorted(pairs.items())) if size > start + 1 else send)
    from_next = jnp.where(even, got[0], got[1])
    from_previous = jnp.where(even, got[1], got[0])
    return from_previous, from_next


def together(*xs):
    return lax.optimization_barrier(xs)


def call(body, outs, scratch=(), passes=1, semaphores=None, **options):
    cells = sum(math.prod(s) for s in scratch[:1])
    sems = [pltpu.SemaphoreType.DMA(semaphores)] if semaphores else []
    return pl.pallas_call(
        body,
        cost_estimate=pl.CostEstimate(flops=16 * passes * cells, bytes_accessed=24 * passes * cells, transcendentals=0),
        out_shape=[jax.ShapeDtypeStruct(s, jnp.float32) for s in outs],
        scratch_shapes=[pltpu.VMEM(s, jnp.float32) for s in scratch] + sems,
        compiler_params=pltpu.CompilerParams(vmem_limit_bytes=48 * 2**20),
        **options,
    )


def cols_kernel(halo, *refs):
    *fields, first_out, last_out = refs
    for k, field in enumerate(fields):
        width = field.shape[1]
        first_out[k] = field[:, :LANES].T[:halo]
        last_out[k] = field[:, width - LANES :].T[LANES - halo :]


def rows_kernel(halo, first_rows, last_rows, left, right, first_out, last_out):
    rows, width = left.shape[-1], first_rows.shape[-1]
    iy, last_iy = lax.axis_index("sy"), lax.axis_size("sy") - 1
    gap = jnp.zeros((LANES - 2 * halo, LANES), jnp.float32)
    for k in range(left.shape[0]):
        for given, out, lane, at in ((first_rows, first_out, 0, 0), (last_rows, last_out, rows - LANES, LANES - halo)):
            after, before = right[k, :, lane : lane + LANES], left[k, :, lane : lane + LANES]
            if k == 0:
                after, before = jnp.where(iy == last_iy, 0.0, after), jnp.where(iy == 0, 0.0, before)
            corners = jnp.concatenate([after, gap, before], axis=0).T
            out[k, :, :width] = given[k * halo : (k + 1) * halo]
            out[k, :, width:] = corners[at : at + halo]


class Grid:
    def __init__(self, rows, width, halo, deep):
        self.rows, self.width, self.halo = rows, width, halo
        self.total, self.wide = rows + 2 * halo, width + LANES
        self.deep = deep
        self.high = round_up(2 * deep, SUBLANES)
        self.strip = (2 * self.high, max(width, rows + LANES))
        self.ext = (self.total, self.wide)
        self.padded = (self.total + 2 * SUBLANES, self.wide)

    def fill(self, dst, tile, before, after, left, right, kap=None, flux=None):
        rows, halo, total, width = self.rows, self.halo, self.total, self.width
        open_rows = 2 * halo - before.shape[0] - after.shape[0]
        gap = [jnp.zeros((open_rows, self.wide), jnp.float32)] if open_rows else []
        dst[rows:total, :] = jnp.concatenate([after, *gap, before], axis=0)
        gap = jnp.zeros((LANES - left.shape[0] - right.shape[0], rows), jnp.float32)
        dst[0:rows, width:] = jnp.concatenate([right, gap, left], axis=0).T
        parts, start = [], 0
        for part in tile:
            parts.append((start, start + part.shape[0], part))
            start += part.shape[0]

        def body(at):
            for first, stop, part in parts:
                lo, hi = max(at.start, first), min(at.stop, stop)
                if lo < hi:
                    dst[lo:hi, 0:width] = part[lo - first : hi - first, :]
            if flux is not None:
                v = dst[at, :]
                return kap[at, :] * v * v

        self.over(body, flux)

    def over(self, body, dst=None):
        total = self.total
        for o in range(0, total, BLOCK):
            size = min(BLOCK, total - o)
            value = body(slice(o, o + size))
            if dst is None:
                continue
            dst[o + SUBLANES : o + SUBLANES + size, :] = value
            if o == 0:
                dst[total + SUBLANES :, :] = value[:SUBLANES]
            if o + size == total:
                dst[0:SUBLANES, :] = value[size - SUBLANES :]

    def lap(self, src, at):
        size, wide = at.stop - at.start, self.wide
        around = src[at.start : at.stop + 2 * SUBLANES, :]
        cur = around[SUBLANES : SUBLANES + size]
        up = pltpu.roll(around, 1, 0)[SUBLANES : SUBLANES + size]
        down = pltpu.roll(around, size + 2 * SUBLANES - 1, 0)[SUBLANES : SUBLANES + size]
        return down + up + pltpu.roll(cur, wide - 1, 1) + pltpu.roll(cur, 1, 1) - 4.0 * cur

    def flux(self, kap, src, dst):
        def body(at):
            v = src[at, :]
            return kap[at, :] * v * v

        self.over(body, dst)

    def first_part(self, kap, w, mid, lap_w, fa, fb, out, more=True, fc=None):
        def one(at):
            lw = self.lap(fa, at)
            lap_w[at, :] = lw
            f = w[at, :] + lw
            return kap[at, :] * f * f

        self.over(one, fb)

        def two(at):
            lw, lf = lap_w[at, :], self.lap(fb, at)
            value = out(at, lf - lw)
            if not more:
                return value
            mid[at, :] = lf - 3.0 * lw
            v = w[at, :] + lw + lf
            return kap[at, :] * v * v

        self.over(two, fa if more else fc)

    def second_part(self, mid, fa, out):
        def one(at):
            out(at, mid[at, :] + 2.0 * self.lap(fa, at))

        self.over(one)


def absorb(grid, kap, point, here, load, even, odd, tail, work, own_only=False):
    wk, mid, lap_w, fa, fb = work
    load(wk, fa)
    step = lax.div(point, 2)

    @pl.when(lax.rem(point, 2) == 1)
    def _():
        def out(at, g):
            odd[step, at, :] = g

        grid.first_part(kap, wk, mid, lap_w, fa, fb, out, False)

    @pl.when(lax.rem(point, 2) == 0)
    def _():
        def out(at, g):
            tail[at, :] = g

        grid.first_part(kap, wk, mid, lap_w, fa, fb, out, not own_only)
        if own_only:
            return

        @pl.when(point < here)
        def _():
            def out(at, h):
                even[step, at, :] = h

            grid.second_part(mid, fa, out)


def start_kernel(
    grid, kappa, initial, before, after, left, right, kap, even, tail, c_out, f_out, wk, low, fa, fb, sems
):
    rows, width = grid.rows, grid.width
    ix, last_ix = lax.axis_index("sx"), lax.axis_size("sx") - 1
    iy, last_iy = lax.axis_index("sy"), lax.axis_size("sy") - 1
    grid.fill(
        kap, [kappa],
        jnp.where(ix == 0, 0.0, before[0]), jnp.where(ix == last_ix, 0.0, after[0]),
        jnp.where(iy == 0, 0.0, left[0]), jnp.where(iy == last_iy, 0.0, right[0]),
    )
    grid.fill(wk, [initial], before[1], after[1], left[1], right[1], kap, fa)

    def one(at):
        f = wk[at, :] + grid.lap(fa, at)
        low[at, :] = f
        return kap[at, :] * f * f

    grid.over(one, fb)

    def two(at):
        v = low[at, :] + grid.lap(fb, at)
        tail[at, :] = v
        return kap[at, :] * v * v

    grid.over(two, fa)
    here = lax.axis_index("tm")
    tile = (slice(0, rows), slice(0, width))
    copies = [
        pltpu.make_async_copy(src.at[tile], dst.at[0], sems.at[i])
        for i, (src, dst) in enumerate(((tail, c_out), (low, f_out)))
    ]

    @pl.when(here == 0)
    def _():
        for copy in copies:
            copy.start()
        for copy in copies:
            copy.wait()

    @pl.when(here > 0)
    def _():
        def three(at):
            even[0, at, :] = tail[at, :] + 2.0 * grid.lap(fa, at)

        grid.over(three)


def loader(grid, kap, tile, strip):
    def load(wk, flux):
        rows, width, deep, high = grid.rows, grid.width, grid.deep, grid.high
        edge = jnp.concatenate([strip[: 2 * deep, :width], strip[high : high + 2 * deep, rows : rows + LANES]], axis=1)
        cols = strip[high : high + 2 * deep, :rows]
        grid.fill(wk, tile, edge[deep:], edge[:deep], cols[deep:], cols[:deep], kap, flux)

    return load


def middle_kernel(grid, bits, kap, even_in, odd_in, tail_in, tile, strip, even, odd, tail, *work):
    here = lax.axis_index("tm")
    point = (here ^ bits) + 1

    @pl.when(point <= here)
    def _():
        absorb(grid, kap, point, here, loader(grid, kap, [tile], strip), even, odd, tail, work)


def last_kernel(
    grid, count, kap, even, odd_in, tail_in, first, second, strip, c_in, f_in, c_out, f_out, odd, tail, *work
):
    wk, mid, lap_w, fa, fb, fc, c_rows, f_rows, sems = work
    here = lax.axis_index("tm")
    point = (here ^ (count - 1)) + 1
    rows, width = grid.rows, grid.width
    load = loader(grid, kap, [first, second], strip)
    state = wk
    chunk = round_up(-(-rows // sems.shape[1]), BLOCK)

    def sent(which, i):
        src, dst = ((c_rows, c_out), (f_rows, f_out))[which]
        part = slice(i * chunk, min((i + 1) * chunk, rows))
        return pltpu.make_async_copy(src.at[part], dst.at[0, part], sems.at[which, i])

    def put(which, at, value):
        stop = min(at.stop, rows)
        if at.start < stop:
            (c_rows, f_rows)[which][at.start : stop, :] = value[: stop - at.start, :width]
            if stop % chunk == 0 or stop == rows:
                sent(which, (stop - 1) // chunk).start()

    @pl.when(here == 1)
    def _():
        def body(at):
            c = tail[at, :]
            put(0, at, even[0, at, :] + odd[0, at, :])
            return kap[at, :] * c * c

        grid.over(body, fa)

        def last(at):
            put(1, at, tail[at, :] + grid.lap(fa, at))

        grid.over(last)

    @pl.when(here >= 2)
    def _():
        @pl.when(point == 1)
        def _():
            load(wk, fa)

            def out(at, g):
                x = even[0, at, :] + g
                state[at, :] = x
                return kap[at, :] * x * x

            grid.first_part(kap, wk, mid, lap_w, fa, fb, out, False, fc)

        @pl.when(point != 1)
        def _():
            @pl.when(point <= here)
            def _():
                absorb(grid, kap, point, here, load, even, odd, tail, work[:5], count == 4)

            def begin(at):
                x = even[0, at, :] + odd[0, at, :]
                state[at, :] = x
                return kap[at, :] * x * x

            grid.over(begin, fc)

        if count > 4:

            def step(j, carry):
                def body(at):
                    x = state[at, :] + 4.0 * grid.lap(fc, at) + (even[j, at, :] + odd[j, at, :])
                    state[at, :] = x
                    return kap[at, :] * x * x

                grid.over(body, fa)
                fc[...] = fa[...]
                return carry

            lax.fori_loop(1, lax.div(here, 2), step, 0)

        @pl.when(lax.rem(here, 2) == 0)
        def _():
            def body(at):
                x, lx = state[at, :], grid.lap(fc, at)
                put(0, at, x + 2.0 * lx + tail[at, :])
                put(1, at, x + lx)

            grid.over(body)

        @pl.when(lax.rem(here, 2) == 1)
        def _():
            j = lax.div(here, 2)

            def body(at):
                x, lx = state[at, :], grid.lap(fc, at)
                c = x + 2.0 * lx + tail[at, :]
                mid[at, :] = c
                put(0, at, x + 4.0 * lx + (even[j, at, :] + odd[j, at, :]))
                return kap[at, :] * c * c

            grid.over(body, fa)

            def last(at):
                put(1, at, mid[at, :] + grid.lap(fa, at))

            grid.over(last)

    @pl.when(here > 0)
    def _():
        for which in (0, 1):
            for i in range(-(-rows // chunk)):
                sent(which, i).wait()


def on_device(initial, kappa, c_guess):
    count = lax.axis_size("tm")
    rows, width = initial.shape
    steps = count // 2
    halo, deep = round_up(steps + 3, SUBLANES), steps + 2
    grid = Grid(rows, width, halo, deep)
    share = round_up(int(rows * SHARE), SUBLANES)
    ext, padded = grid.ext, grid.padded
    work = [ext] * 3 + [padded] * 2
    sides = (steps, *ext)

    tiles, strips = {0: c_guess[0]}, {}
    singles = [1 << i for i in range((count - 1).bit_length())]
    several = sorted((d for d in range(1, count - 1) if d not in singles), key=lambda d: d.bit_count())
    for bit in singles:
        if bit < count - 1:
            tiles[bit] = swap(c_guess, "tm", bit)[0]

    fields = (kappa, initial, c_guess[0])
    packed = (len(fields), halo, rows)
    first_cols, last_cols = call(functools.partial(cols_kernel, halo), [packed] * 2)(
        kappa, initial, jnp.concatenate([c_guess[0, :, :LANES], c_guess[0, :, width - LANES :]], axis=1)
    )
    left, right = neighbours("sy", last_cols, first_cols)
    packed = (len(fields), halo, grid.wide)
    first_rows, last_rows = call(functools.partial(rows_kernel, halo), [packed] * 2)(
        jnp.concatenate([x[:halo] for x in fields], axis=0),
        jnp.concatenate([x[rows - halo :] for x in fields], axis=0),
        left, right,
    )
    before, after = neighbours("sx", last_rows, first_rows)

    def padded_to(x, shape):
        return jnp.pad(x, [(0, n - m) for m, n in zip(x.shape, shape)])

    part = (grid.high, grid.strip[1])
    edge = jnp.concatenate([after[2, :deep], before[2, halo - deep :]], axis=0)
    cols = jnp.concatenate([right[2, :deep], left[2, halo - deep :]], axis=0)
    strip = jnp.concatenate(
        [padded_to(edge[:, :width], part), padded_to(jnp.concatenate([cols, edge[:, width:]], axis=1), part)], axis=0
    )
    strips[0] = strip
    for bit in singles:
        if bit < count - 1:
            strips[bit] = swap(strip, "tm", bit)

    before, strip = together(before, strip)
    outside, inside = pl.BlockSpec(memory_space=pltpu.HBM), pl.BlockSpec(memory_space=pltpu.VMEM)
    kap, even, tail, c_new, f_new = call(
        functools.partial(start_kernel, grid), [ext, sides, ext] + [c_guess.shape] * 2, [ext] * 2 + [padded] * 2, 4,
        semaphores=(2,), out_specs=[inside] * 3 + [outside] * 2,
    )(kappa, initial, before, after, left, right)
    odd = jnp.zeros(sides, jnp.float32)

    for d in several:
        bit = d & -d
        tiles[d], strips[d] = swap(tiles[d ^ bit], "tm", bit), swap(strips[d ^ bit], "tm", bit)
    near, far, last = singles[0], singles[-1], count - 1
    first, second = swap(tiles[last ^ near][:share], "tm", near), swap(tiles[last ^ far][share:], "tm", far)
    strips[last] = swap(strips[last ^ near], "tm", near)
    for d in (*singles, *several):
        if d != last:
            even, odd, tail = call(
                functools.partial(middle_kernel, grid, d), [sides, sides, ext], work, MIDDLE,
                input_output_aliases={1: 0, 2: 1, 3: 2},
            )(kap, even, odd, tail, tiles[d], strips[d])
    c_new, f_new, _, _ = call(
        functools.partial(last_kernel, grid, count), [c_guess.shape] * 2 + [sides, ext],
        work + [padded] + [(rows, width)] * 2, 8, semaphores=(2, CHUNKS), input_output_aliases={2: 2, 3: 3, 7: 0, 8: 1},
        in_specs=[inside] * 7 + [outside] * 2, out_specs=[outside] * 2 + [inside] * 2,
    )(kap, even, odd, tail, first, second, strips[last], c_new, f_new)
    return c_new, f_new


def solution(mesh):
    return jax.shard_map(
        on_device,
        mesh=mesh,
        in_specs=(P("sx", "sy"), P("sx", "sy"), P("tm", "sx", "sy")),
        out_specs=(P("tm", "sx", "sy"), P("tm", "sx", "sy")),
        check_vma=False,
    )
```

```python
import functools
import math
import jax
import jax.numpy as jnp
from jax import lax
from jax.experimental import pallas as pl
from jax.experimental.pallas import tpu as pltpu
from jax.sharding import PartitionSpec as P

LANES = 128
SUBLANES = 8
BLOCK = 16
CHUNKS = 4
SHARE = 15 / 32
MIDDLE = 430


def round_up(value, step):
    return -(-value // step) * step


def swap(x, axis, bits):
    return lax.ppermute(x, axis, [(i, i ^ bits) for i in range(lax.axis_size(axis))])


def neighbours(axis, to_next, to_previous):
    size, index = lax.axis_size(axis), lax.axis_index(axis)
    even = index % 2 == 0
    got = []
    for start in (0, 1):
        pairs = {i: i for i in range(size)}
        for i in range(start, size - 1, 2):
            pairs[i], pairs[i + 1] = i + 1, i
        send = jnp.where(even == (start == 0), to_next, to_previous)
        got.append(lax.ppermute(send, axis, sorted(pairs.items())) if size > start + 1 else send)
    from_next = jnp.where(even, got[0], got[1])
    from_previous = jnp.where(even, got[1], got[0])
    return from_previous, from_next


def together(*xs):
    return lax.optimization_barrier(xs)


def call(body, outs, scratch=(), passes=1, semaphores=None, **options):
    cells = sum(math.prod(s) for s in scratch[:1])
    sems = [pltpu.SemaphoreType.DMA(semaphores)] if semaphores else []
    return pl.pallas_call(
        body,
        cost_estimate=pl.CostEstimate(flops=16 * passes * cells, bytes_accessed=24 * passes * cells, transcendentals=0),
        out_shape=[jax.ShapeDtypeStruct(s, jnp.float32) for s in outs],
        scratch_shapes=[pltpu.VMEM(s, jnp.float32) for s in scratch] + sems,
        compiler_params=pltpu.CompilerParams(vmem_limit_bytes=48 * 2**20),
        **options,
    )


def cols_kernel(halo, *refs):
    *fields, first_out, last_out = refs
    for k, field in enumerate(fields):
        width = field.shape[1]
        first_out[k] = field[:, :LANES].T[:halo]
        last_out[k] = field[:, width - LANES :].T[LANES - halo :]


def rows_kernel(halo, first_rows, last_rows, left, right, first_out, last_out):
    rows, width = left.shape[-1], first_rows.shape[-1]
    iy, last_iy = lax.axis_index("sy"), lax.axis_size("sy") - 1
    gap = jnp.zeros((LANES - 2 * halo, LANES), jnp.float32)
    for k in range(left.shape[0]):
        for given, out, lane, at in ((first_rows, first_out, 0, 0), (last_rows, last_out, rows - LANES, LANES - halo)):
            after, before = right[k, :, lane : lane + LANES], left[k, :, lane : lane + LANES]
            if k == 0:
                after, before = jnp.where(iy == last_iy, 0.0, after), jnp.where(iy == 0, 0.0, before)
            corners = jnp.concatenate([after, gap, before], axis=0).T
            out[k, :, :width] = given[k * halo : (k + 1) * halo]
            out[k, :, width:] = corners[at : at + halo]


class Grid:
    def __init__(self, rows, width, halo, deep):
        self.rows, self.width, self.halo = rows, width, halo
        self.total, self.wide = rows + 2 * halo, width + LANES
        self.deep = deep
        self.high = round_up(2 * deep, SUBLANES)
        self.strip = (2 * self.high, max(width, rows + LANES))
        self.ext = (self.total, self.wide)
        self.padded = (self.total + 2 * SUBLANES, self.wide)

    def fill(self, dst, tile, before, after, left, right, kap=None, flux=None):
        rows, halo, total, width = self.rows, self.halo, self.total, self.width
        open_rows = 2 * halo - before.shape[0] - after.shape[0]
        gap = [jnp.zeros((open_rows, self.wide), jnp.float32)] if open_rows else []
        dst[rows:total, :] = jnp.concatenate([after, *gap, before], axis=0)
        gap = jnp.zeros((LANES - left.shape[0] - right.shape[0], rows), jnp.float32)
        dst[0:rows, width:] = jnp.concatenate([right, gap, left], axis=0).T
        parts, start = [], 0
        for part in tile:
            parts.append((start, start + part.shape[0], part))
            start += part.shape[0]

        def body(at):
            for first, stop, part in parts:
                lo, hi = max(at.start, first), min(at.stop, stop)
                if lo < hi:
                    dst[lo:hi, 0:width] = part[lo - first : hi - first, :]
            if flux is not None:
                v = dst[at, :]
                return kap[at, :] * v * v

        self.over(body, flux)

    def over(self, body, dst=None):
        total = self.total
        for o in range(0, total, BLOCK):
            size = min(BLOCK, total - o)
            value = body(slice(o, o + size))
            if dst is None:
                continue
            dst[o + SUBLANES : o + SUBLANES + size, :] = value
            if o == 0:
                dst[total + SUBLANES :, :] = value[:SUBLANES]
            if o + size == total:
                dst[0:SUBLANES, :] = value[size - SUBLANES :]

    def lap(self, src, at):
        size, wide = at.stop - at.start, self.wide
        around = src[at.start : at.stop + 2 * SUBLANES, :]
        cur = around[SUBLANES : SUBLANES + size]
        up = pltpu.roll(around, 1, 0)[SUBLANES : SUBLANES + size]
        down = pltpu.roll(around, size + 2 * SUBLANES - 1, 0)[SUBLANES : SUBLANES + size]
        return down + up + pltpu.roll(cur, wide - 1, 1) + pltpu.roll(cur, 1, 1) - 4.0 * cur

    def flux(self, kap, src, dst):
        def body(at):
            v = src[at, :]
            return kap[at, :] * v * v

        self.over(body, dst)

    def first_part(self, kap, w, mid, lap_w, fa, fb, out, more=True, fc=None):
        def one(at):
            lw = self.lap(fa, at)
            lap_w[at, :] = lw
            f = w[at, :] + lw
            return kap[at, :] * f * f

        self.over(one, fb)

        def two(at):
            lw, lf = lap_w[at, :], self.lap(fb, at)
            value = out(at, lf - lw)
            if not more:
                return value
            mid[at, :] = lf - 3.0 * lw
            v = w[at, :] + lw + lf
            return kap[at, :] * v * v

        self.over(two, fa if more else fc)

    def second_part(self, mid, fa, out):
        def one(at):
            out(at, mid[at, :] + 2.0 * self.lap(fa, at))

        self.over(one)


def absorb(grid, kap, point, here, load, even, odd, tail, work, own_only=False):
    wk, mid, lap_w, fa, fb = work
    load(wk, fa)
    step = lax.div(point, 2)

    @pl.when(lax.rem(point, 2) == 1)
    def _():
        def out(at, g):
            odd[step, at, :] = g

        grid.first_part(kap, wk, mid, lap_w, fa, fb, out, False)

    @pl.when(lax.rem(point, 2) == 0)
    def _():
        def out(at, g):
            tail[at, :] = g if lax.axis_size("tm") <= 4 else jnp.where(step == lax.div(here, 2), g, tail[at, :])

        grid.first_part(kap, wk, mid, lap_w, fa, fb, out, not own_only)
        if own_only:
            return

        @pl.when(point < here)
        def _():
            def out(at, h):
                even[step, at, :] = h

            grid.second_part(mid, fa, out)


def start_kernel(
    grid, kappa, initial, before, after, left, right, kap, even, tail, c_out, f_out, wk, low, fa, fb, sems
):
    rows, width = grid.rows, grid.width
    ix, last_ix = lax.axis_index("sx"), lax.axis_size("sx") - 1
    iy, last_iy = lax.axis_index("sy"), lax.axis_size("sy") - 1
    grid.fill(
        kap, [kappa],
        jnp.where(ix == 0, 0.0, before[0]), jnp.where(ix == last_ix, 0.0, after[0]),
        jnp.where(iy == 0, 0.0, left[0]), jnp.where(iy == last_iy, 0.0, right[0]),
    )
    grid.fill(wk, [initial], before[1], after[1], left[1], right[1], kap, fa)

    def one(at):
        f = wk[at, :] + grid.lap(fa, at)
        low[at, :] = f
        return kap[at, :] * f * f

    grid.over(one, fb)

    def two(at):
        v = low[at, :] + grid.lap(fb, at)
        tail[at, :] = v
        return kap[at, :] * v * v

    grid.over(two, fa)
    here = lax.axis_index("tm")
    tile = (slice(0, rows), slice(0, width))
    copies = [
        pltpu.make_async_copy(src.at[tile], dst.at[0], sems.at[i])
        for i, (src, dst) in enumerate(((tail, c_out), (low, f_out)))
    ]

    @pl.when(here == 0)
    def _():
        for copy in copies:
            copy.start()
        for copy in copies:
            copy.wait()

    @pl.when(here > 0)
    def _():
        def three(at):
            even[0, at, :] = tail[at, :] + 2.0 * grid.lap(fa, at)

        grid.over(three)


def loader(grid, kap, tile, strip):
    def load(wk, flux):
        rows, width, deep, high = grid.rows, grid.width, grid.deep, grid.high
        edge = jnp.concatenate([strip[: 2 * deep, :width], strip[high : high + 2 * deep, rows : rows + LANES]], axis=1)
        cols = strip[high : high + 2 * deep, :rows]
        grid.fill(wk, tile, edge[deep:], edge[:deep], cols[deep:], cols[:deep], kap, flux)

    return load


def middle_kernel(grid, bits, kap, even_in, odd_in, tail_in, tile, strip, even, odd, tail, *work):
    here = lax.axis_index("tm")
    point = (here ^ bits) + 1
    even[...], odd[...], tail[...] = even_in[...], odd_in[...], tail_in[...]

    @pl.when(point <= here)
    def _():
        absorb(grid, kap, point, here, loader(grid, kap, [tile], strip), even, odd, tail, work)


def last_kernel(grid, count, kap, even, odd, tail, first, second, strip, c_in, f_in, c_out, f_out, *work):
    wk, mid, lap_w, fa, fb, fc, c_rows, f_rows, even_own, odd_own, tail_own, sems = work
    here = lax.axis_index("tm")
    point = (here ^ (count - 1)) + 1
    rows, width = grid.rows, grid.width
    load = loader(grid, kap, [first, second], strip)
    state = wk
    tail_even = tail_own
    if count != 4:
        even_own[...], odd_own[...], tail_own[...] = even[...], odd[...], tail[...]
        even, odd, tail = even_own, odd_own, tail_own
    if count == 2:

        @pl.when(here == 1)
        def _():
            absorb(grid, kap, point, here, load, even, odd, tail, work[:5])

    chunk = round_up(-(-rows // sems.shape[1]), BLOCK)

    def sent(which, i):
        src, dst = ((c_rows, c_out), (f_rows, f_out))[which]
        part = slice(i * chunk, min((i + 1) * chunk, rows))
        return pltpu.make_async_copy(src.at[part], dst.at[0, part], sems.at[which, i])

    def put(which, at, value):
        stop = min(at.stop, rows)
        if at.start < stop:
            (c_rows, f_rows)[which][at.start : stop, :] = value[: stop - at.start, :width]
            if stop % chunk == 0 or stop == rows:
                sent(which, (stop - 1) // chunk).start()

    @pl.when(here == 1)
    def _():
        def body(at):
            c = tail[at, :]
            put(0, at, even[0, at, :] + odd[0, at, :])
            return kap[at, :] * c * c

        grid.over(body, fa)

        def last(at):
            put(1, at, tail[at, :] + grid.lap(fa, at))

        grid.over(last)

    @pl.when(here >= 2)
    def _():
        @pl.when(point == 1)
        def _():
            load(wk, fa)

            def out(at, g):
                x = even[0, at, :] + g
                state[at, :] = x
                return kap[at, :] * x * x

            grid.first_part(kap, wk, mid, lap_w, fa, fb, out, False, fc)

        @pl.when(point != 1)
        def _():
            @pl.when(point <= here)
            def _():
                absorb(grid, kap, point, here, load, even, odd_own, tail_own, work[:5], count == 4)

            def begin(at):
                x = even[0, at, :] + odd[0, at, :]
                state[at, :] = x
                return kap[at, :] * x * x

            grid.over(begin, fc)

        if count > 4:

            def step(j, carry):
                def body(at):
                    x = state[at, :] + 4.0 * grid.lap(fc, at) + (even[j, at, :] + odd[j, at, :])
                    state[at, :] = x
                    return kap[at, :] * x * x

                grid.over(body, fa)
                fc[...] = fa[...]
                return carry

            lax.fori_loop(1, lax.div(here, 2), step, 0)

        @pl.when(lax.rem(here, 2) == 0)
        def _():
            def body(at):
                x, lx = state[at, :], grid.lap(fc, at)
                put(0, at, x + 2.0 * lx + tail_even[at, :])
                put(1, at, x + lx)

            grid.over(body)

        @pl.when(lax.rem(here, 2) == 1)
        def _():
            j = lax.div(here, 2)

            def body(at):
                x, lx = state[at, :], grid.lap(fc, at)
                c = x + 2.0 * lx + tail[at, :]
                mid[at, :] = c
                put(0, at, x + 4.0 * lx + (even[j, at, :] + odd[j, at, :]))
                return kap[at, :] * c * c

            grid.over(body, fa)

            def last(at):
                put(1, at, mid[at, :] + grid.lap(fa, at))

            grid.over(last)

    @pl.when(here > 0)
    def _():
        for which in (0, 1):
            for i in range(-(-rows // chunk)):
                sent(which, i).wait()


def on_device(initial, kappa, c_guess):
    count = lax.axis_size("tm")
    rows, width = initial.shape
    steps = count // 2
    halo, deep = round_up(steps + 3, SUBLANES), steps + 2
    grid = Grid(rows, width, halo, deep)
    share = round_up(int(rows * SHARE), SUBLANES)
    ext, padded = grid.ext, grid.padded
    work = [ext] * 3 + [padded] * 2
    sides = (steps, *ext)

    tiles, strips = {0: c_guess[0]}, {}
    singles = [1 << i for i in range((count - 1).bit_length())]
    several = sorted((d for d in range(1, count - 1) if d not in singles), key=lambda d: d.bit_count())
    for bit in singles:
        if bit < count - 1:
            tiles[bit] = swap(c_guess, "tm", bit)[0]

    fields = (kappa, initial, c_guess[0])
    packed = (len(fields), halo, rows)
    first_cols, last_cols = call(functools.partial(cols_kernel, halo), [packed] * 2)(
        kappa, initial, jnp.concatenate([c_guess[0, :, :LANES], c_guess[0, :, width - LANES :]], axis=1)
    )
    left, right = neighbours("sy", last_cols, first_cols)
    packed = (len(fields), halo, grid.wide)
    first_rows, last_rows = call(functools.partial(rows_kernel, halo), [packed] * 2)(
        jnp.concatenate([x[:halo] for x in fields], axis=0),
        jnp.concatenate([x[rows - halo :] for x in fields], axis=0),
        left, right,
    )
    before, after = neighbours("sx", last_rows, first_rows)

    def padded_to(x, shape):
        return jnp.pad(x, [(0, n - m) for m, n in zip(x.shape, shape)])

    part = (grid.high, grid.strip[1])
    edge = jnp.concatenate([after[2, :deep], before[2, halo - deep :]], axis=0)
    cols = jnp.concatenate([right[2, :deep], left[2, halo - deep :]], axis=0)
    strip = jnp.concatenate(
        [padded_to(edge[:, :width], part), padded_to(jnp.concatenate([cols, edge[:, width:]], axis=1), part)], axis=0
    )
    strips[0] = strip
    for bit in singles:
        if bit < count - 1:
            strips[bit] = swap(strip, "tm", bit)

    before, strip = together(before, strip)
    outside, inside = pl.BlockSpec(memory_space=pltpu.HBM), pl.BlockSpec(memory_space=pltpu.VMEM)
    kap, even, tail, c_new, f_new = call(
        functools.partial(start_kernel, grid), [ext, sides, ext] + [c_guess.shape] * 2, [ext] * 2 + [padded] * 2, 4,
        semaphores=(2,), out_specs=[inside] * 3 + [outside] * 2,
    )(kappa, initial, before, after, left, right)
    odd = jnp.zeros(sides, jnp.float32)

    for d in several:
        bit = d & -d
        tiles[d], strips[d] = swap(tiles[d ^ bit], "tm", bit), swap(strips[d ^ bit], "tm", bit)
    near, far, last = singles[0], singles[-1], count - 1
    first, second = swap(tiles[last ^ near][:share], "tm", near), swap(tiles[last ^ far][share:], "tm", far)
    strips[last] = swap(strips[last ^ near], "tm", near)
    for d in (*singles, *several):
        if d != last:
            even, odd, tail = call(
                functools.partial(middle_kernel, grid, d), [sides, sides, ext], work, MIDDLE,
                input_output_aliases={1: 0, 2: 1, 3: 2},
            )(kap, even, odd, tail, tiles[d], strips[d])
    own = [sides, sides, ext] if count != 4 else [(1, *grid.ext), (1, *grid.ext), ext]
    c_new, f_new = call(
        functools.partial(last_kernel, grid, count), [c_guess.shape] * 2, work + [padded] + [(rows, width)] * 2 + own, 8,
        semaphores=(2, CHUNKS), input_output_aliases={7: 0, 8: 1},
        in_specs=[inside] * 7 + [outside] * 2, out_specs=[outside] * 2,
    )(kap, even, odd, tail, first, second, strips[last], c_new, f_new)
    return c_new, f_new


def solution(mesh):
    return jax.shard_map(
        on_device,
        mesh=mesh,
        in_specs=(P("sx", "sy"), P("sx", "sy"), P("tm", "sx", "sy")),
        out_specs=(P("tm", "sx", "sy"), P("tm", "sx", "sy")),
        check_vma=False,
    )
```

```python
import functools
import math
import jax
import jax.numpy as jnp
from jax import lax
from jax.experimental import pallas as pl
from jax.experimental.pallas import tpu as pltpu
from jax.sharding import PartitionSpec as P

LANES = 128
SUBLANES = 8
BLOCK = 16
CHUNKS = (1 / 2, 7 / 8, 1)
SHARE = 15 / 32
MIDDLE = 430


def round_up(value, step):
    return -(-value // step) * step


def swap(x, axis, bits):
    return lax.ppermute(x, axis, [(i, i ^ bits) for i in range(lax.axis_size(axis))])


def neighbours(axis, to_next, to_previous):
    size, index = lax.axis_size(axis), lax.axis_index(axis)
    even = index % 2 == 0
    got = []
    for start in (0, 1):
        pairs = {i: i for i in range(size)}
        for i in range(start, size - 1, 2):
            pairs[i], pairs[i + 1] = i + 1, i
        send = jnp.where(even == (start == 0), to_next, to_previous)
        got.append(lax.ppermute(send, axis, sorted(pairs.items())) if size > start + 1 else send)
    from_next = jnp.where(even, got[0], got[1])
    from_previous = jnp.where(even, got[1], got[0])
    return from_previous, from_next


def together(*xs):
    return lax.optimization_barrier(xs)


def call(body, outs, scratch=(), passes=1, semaphores=None, **options):
    cells = sum(math.prod(s) for s in scratch[:1])
    sems = [pltpu.SemaphoreType.DMA(semaphores)] if semaphores else []
    return pl.pallas_call(
        body,
        cost_estimate=pl.CostEstimate(flops=16 * passes * cells, bytes_accessed=24 * passes * cells, transcendentals=0),
        out_shape=[jax.ShapeDtypeStruct(s, jnp.float32) for s in outs],
        scratch_shapes=[pltpu.VMEM(s, jnp.float32) for s in scratch] + sems,
        compiler_params=pltpu.CompilerParams(vmem_limit_bytes=48 * 2**20),
        **options,
    )


def cols_kernel(halo, *refs):
    *fields, first_out, last_out = refs
    for k, field in enumerate(fields):
        width = field.shape[1]
        first_out[k] = field[:, :LANES].T[:halo]
        last_out[k] = field[:, width - LANES :].T[LANES - halo :]


def rows_kernel(halo, first_rows, last_rows, left, right, first_out, last_out):
    rows, width = left.shape[-1], first_rows.shape[-1]
    iy, last_iy = lax.axis_index("sy"), lax.axis_size("sy") - 1
    gap = jnp.zeros((LANES - 2 * halo, LANES), jnp.float32)
    for k in range(left.shape[0]):
        for given, out, lane, at in ((first_rows, first_out, 0, 0), (last_rows, last_out, rows - LANES, LANES - halo)):
            after, before = right[k, :, lane : lane + LANES], left[k, :, lane : lane + LANES]
            if k == 0:
                after, before = jnp.where(iy == last_iy, 0.0, after), jnp.where(iy == 0, 0.0, before)
            corners = jnp.concatenate([after, gap, before], axis=0).T
            out[k, :, :width] = given[k * halo : (k + 1) * halo]
            out[k, :, width:] = corners[at : at + halo]


class Grid:
    def __init__(self, rows, width, halo, deep):
        self.rows, self.width, self.halo = rows, width, halo
        self.total, self.wide = rows + 2 * halo, width + LANES
        self.deep = deep
        self.high = round_up(2 * deep, SUBLANES)
        self.strip = (2 * self.high, max(width, rows + LANES))
        self.ext = (self.total, self.wide)
        self.padded = (self.total + 2 * SUBLANES, self.wide)

    def fill(self, dst, tile, before, after, left, right, kap=None, flux=None):
        rows, halo, total, width = self.rows, self.halo, self.total, self.width
        open_rows = 2 * halo - before.shape[0] - after.shape[0]
        gap = [jnp.zeros((open_rows, self.wide), jnp.float32)] if open_rows else []
        dst[rows:total, :] = jnp.concatenate([after, *gap, before], axis=0)
        gap = jnp.zeros((LANES - left.shape[0] - right.shape[0], rows), jnp.float32)
        dst[0:rows, width:] = jnp.concatenate([right, gap, left], axis=0).T
        parts, start = [], 0
        for part in tile:
            parts.append((start, start + part.shape[0], part))
            start += part.shape[0]

        def body(at):
            for first, stop, part in parts:
                lo, hi = max(at.start, first), min(at.stop, stop)
                if lo < hi:
                    dst[lo:hi, 0:width] = part[lo - first : hi - first, :]
            if flux is not None:
                v = dst[at, :]
                return kap[at, :] * v * v

        self.over(body, flux)

    def over(self, body, dst=None):
        total = self.total
        for o in range(0, total, BLOCK):
            size = min(BLOCK, total - o)
            value = body(slice(o, o + size))
            if dst is None:
                continue
            dst[o + SUBLANES : o + SUBLANES + size, :] = value
            if o == 0:
                dst[total + SUBLANES :, :] = value[:SUBLANES]
            if o + size == total:
                dst[0:SUBLANES, :] = value[size - SUBLANES :]

    def lap(self, src, at):
        size, wide = at.stop - at.start, self.wide
        around = src[at.start : at.stop + 2 * SUBLANES, :]
        cur = around[SUBLANES : SUBLANES + size]
        up = pltpu.roll(around, 1, 0)[SUBLANES : SUBLANES + size]
        down = pltpu.roll(around, size + 2 * SUBLANES - 1, 0)[SUBLANES : SUBLANES + size]
        return down + up + pltpu.roll(cur, wide - 1, 1) + pltpu.roll(cur, 1, 1) - 4.0 * cur

    def flux(self, kap, src, dst):
        def body(at):
            v = src[at, :]
            return kap[at, :] * v * v

        self.over(body, dst)

    def first_part(self, kap, w, mid, lap_w, fa, fb, out, more=True, fc=None):
        def one(at):
            lw = self.lap(fa, at)
            lap_w[at, :] = lw
            f = w[at, :] + lw
            return kap[at, :] * f * f

        self.over(one, fb)

        def two(at):
            lw, lf = lap_w[at, :], self.lap(fb, at)
            value = out(at, lf - lw)
            if not more:
                return value
            mid[at, :] = lf - 3.0 * lw
            v = w[at, :] + lw + lf
            return kap[at, :] * v * v

        self.over(two, fa if more else fc)

    def second_part(self, mid, fa, out):
        def one(at):
            out(at, mid[at, :] + 2.0 * self.lap(fa, at))

        self.over(one)


def absorb(grid, kap, point, here, load, even, odd, tail, work, own_only=False):
    wk, mid, lap_w, fa, fb = work
    load(wk, fa)
    step = lax.div(point, 2)

    @pl.when(lax.rem(point, 2) == 1)
    def _():
        def out(at, g):
            odd[step, at, :] = g

        grid.first_part(kap, wk, mid, lap_w, fa, fb, out, False)

    @pl.when(lax.rem(point, 2) == 0)
    def _():
        def out(at, g):
            tail[at, :] = g if lax.axis_size("tm") <= 4 else jnp.where(step == lax.div(here, 2), g, tail[at, :])

        grid.first_part(kap, wk, mid, lap_w, fa, fb, out, not own_only)
        if own_only:
            return

        @pl.when(point < here)
        def _():
            def out(at, h):
                even[step, at, :] = h

            grid.second_part(mid, fa, out)


def start_kernel(
    grid, kappa, initial, before, after, left, right, kap, even, tail, c_out, f_out, wk, low, fa, fb, sems
):
    rows, width = grid.rows, grid.width
    ix, last_ix = lax.axis_index("sx"), lax.axis_size("sx") - 1
    iy, last_iy = lax.axis_index("sy"), lax.axis_size("sy") - 1
    grid.fill(
        kap, [kappa],
        jnp.where(ix == 0, 0.0, before[0]), jnp.where(ix == last_ix, 0.0, after[0]),
        jnp.where(iy == 0, 0.0, left[0]), jnp.where(iy == last_iy, 0.0, right[0]),
    )
    grid.fill(wk, [initial], before[1], after[1], left[1], right[1], kap, fa)

    def one(at):
        f = wk[at, :] + grid.lap(fa, at)
        low[at, :] = f
        return kap[at, :] * f * f

    grid.over(one, fb)

    def two(at):
        v = low[at, :] + grid.lap(fb, at)
        tail[at, :] = v
        return kap[at, :] * v * v

    grid.over(two, fa)
    here = lax.axis_index("tm")
    tile = (slice(0, rows), slice(0, width))
    copies = [
        pltpu.make_async_copy(src.at[tile], dst.at[0], sems.at[i])
        for i, (src, dst) in enumerate(((tail, c_out), (low, f_out)))
    ]

    @pl.when(here == 0)
    def _():
        for copy in copies:
            copy.start()
        for copy in copies:
            copy.wait()

    @pl.when(here > 0)
    def _():
        def three(at):
            even[0, at, :] = tail[at, :] + 2.0 * grid.lap(fa, at)

        grid.over(three)


def loader(grid, kap, tile, strip):
    def load(wk, flux):
        rows, width, deep, high = grid.rows, grid.width, grid.deep, grid.high
        edge = jnp.concatenate([strip[: 2 * deep, :width], strip[high : high + 2 * deep, rows : rows + LANES]], axis=1)
        cols = strip[high : high + 2 * deep, :rows]
        grid.fill(wk, tile, edge[deep:], edge[:deep], cols[deep:], cols[:deep], kap, flux)

    return load


def middle_kernel(grid, bits, kap, even_in, odd_in, tail_in, tile, strip, even, odd, tail, *work):
    here = lax.axis_index("tm")
    point = (here ^ bits) + 1
    even[...], odd[...], tail[...] = even_in[...], odd_in[...], tail_in[...]

    @pl.when(point <= here)
    def _():
        absorb(grid, kap, point, here, loader(grid, kap, [tile], strip), even, odd, tail, work)


def last_kernel(grid, count, kap, even, odd, tail, first, second, strip, c_in, f_in, c_out, f_out, *work):
    wk, mid, lap_w, fa, fb, fc, c_rows, f_rows, even_own, odd_own, tail_own, sems = work
    here = lax.axis_index("tm")
    point = (here ^ (count - 1)) + 1
    rows, width = grid.rows, grid.width
    load = loader(grid, kap, [first, second], strip)
    state = wk
    tail_even = tail_own
    if count != 4:
        even_own[...], odd_own[...], tail_own[...] = even[...], odd[...], tail[...]
        even, odd, tail = even_own, odd_own, tail_own
    if count == 2:

        @pl.when(here == 1)
        def _():
            absorb(grid, kap, point, here, load, even, odd, tail, work[:5])

    stops = sorted({min(rows, round_up(int(rows * part), BLOCK)) for part in CHUNKS})

    def sent(which, i):
        src, dst = ((c_rows, c_out), (f_rows, f_out))[which]
        part = slice(stops[i - 1] if i else 0, stops[i])
        return pltpu.make_async_copy(src.at[part], dst.at[0, part], sems.at[which, i])

    def put(which, at, value):
        stop = min(at.stop, rows)
        if at.start < stop:
            (c_rows, f_rows)[which][at.start : stop, :] = value[: stop - at.start, :width]
            if stop in stops:
                sent(which, stops.index(stop)).start()

    @pl.when(here == 1)
    def _():
        def body(at):
            c = tail[at, :]
            put(0, at, even[0, at, :] + odd[0, at, :])
            return kap[at, :] * c * c

        grid.over(body, fa)

        def last(at):
            put(1, at, tail[at, :] + grid.lap(fa, at))

        grid.over(last)

    @pl.when(here >= 2)
    def _():
        @pl.when(point == 1)
        def _():
            load(wk, fa)

            def out(at, g):
                x = even[0, at, :] + g
                state[at, :] = x
                return kap[at, :] * x * x

            grid.first_part(kap, wk, mid, lap_w, fa, fb, out, False, fc)

        @pl.when(point != 1)
        def _():
            @pl.when(point <= here)
            def _():
                absorb(grid, kap, point, here, load, even, odd_own, tail_own, work[:5], count == 4)

            def begin(at):
                x = even[0, at, :] + odd[0, at, :]
                state[at, :] = x
                return kap[at, :] * x * x

            grid.over(begin, fc)

        if count > 4:

            def step(j, carry):
                def body(at):
                    x = state[at, :] + 4.0 * grid.lap(fc, at) + (even[j, at, :] + odd[j, at, :])
                    state[at, :] = x
                    return kap[at, :] * x * x

                grid.over(body, fa)
                fc[...] = fa[...]
                return carry

            lax.fori_loop(1, lax.div(here, 2), step, 0)

        @pl.when(lax.rem(here, 2) == 0)
        def _():
            def body(at):
                x, lx = state[at, :], grid.lap(fc, at)
                put(0, at, x + 2.0 * lx + tail_even[at, :])
                put(1, at, x + lx)

            grid.over(body)

        @pl.when(lax.rem(here, 2) == 1)
        def _():
            j = lax.div(here, 2)

            def body(at):
                x, lx = state[at, :], grid.lap(fc, at)
                c = x + 2.0 * lx + tail[at, :]
                mid[at, :] = c
                put(0, at, x + 4.0 * lx + (even[j, at, :] + odd[j, at, :]))
                return kap[at, :] * c * c

            grid.over(body, fa)

            def last(at):
                put(1, at, mid[at, :] + grid.lap(fa, at))

            grid.over(last)

    @pl.when(here > 0)
    def _():
        for which in (0, 1):
            for i in range(len(stops)):
                sent(which, i).wait()


def on_device(initial, kappa, c_guess):
    count = lax.axis_size("tm")
    rows, width = initial.shape
    steps = count // 2
    halo, deep = round_up(steps + 3, SUBLANES), steps + 2
    grid = Grid(rows, width, halo, deep)
    share = round_up(int(rows * SHARE), SUBLANES)
    ext, padded = grid.ext, grid.padded
    work = [ext] * 3 + [padded] * 2
    sides = (steps, *ext)

    tiles, strips = {0: c_guess[0]}, {}
    singles = [1 << i for i in range((count - 1).bit_length())]
    several = sorted((d for d in range(1, count - 1) if d not in singles), key=lambda d: d.bit_count())
    for bit in singles:
        if bit < count - 1:
            tiles[bit] = swap(c_guess, "tm", bit)[0]

    fields = (kappa, initial, c_guess[0])
    packed = (len(fields), halo, rows)
    first_cols, last_cols = call(functools.partial(cols_kernel, halo), [packed] * 2)(
        kappa, initial, jnp.concatenate([c_guess[0, :, :LANES], c_guess[0, :, width - LANES :]], axis=1)
    )
    left, right = neighbours("sy", last_cols, first_cols)
    packed = (len(fields), halo, grid.wide)
    first_rows, last_rows = call(functools.partial(rows_kernel, halo), [packed] * 2)(
        jnp.concatenate([x[:halo] for x in fields], axis=0),
        jnp.concatenate([x[rows - halo :] for x in fields], axis=0),
        left, right,
    )
    before, after = neighbours("sx", last_rows, first_rows)

    def padded_to(x, shape):
        return jnp.pad(x, [(0, n - m) for m, n in zip(x.shape, shape)])

    part = (grid.high, grid.strip[1])
    edge = jnp.concatenate([after[2, :deep], before[2, halo - deep :]], axis=0)
    cols = jnp.concatenate([right[2, :deep], left[2, halo - deep :]], axis=0)
    strip = jnp.concatenate(
        [padded_to(edge[:, :width], part), padded_to(jnp.concatenate([cols, edge[:, width:]], axis=1), part)], axis=0
    )
    strips[0] = strip
    for bit in singles:
        if bit < count - 1:
            strips[bit] = swap(strip, "tm", bit)

    before, strip = together(before, strip)
    outside, inside = pl.BlockSpec(memory_space=pltpu.HBM), pl.BlockSpec(memory_space=pltpu.VMEM)
    kap, even, tail, c_new, f_new = call(
        functools.partial(start_kernel, grid), [ext, sides, ext] + [c_guess.shape] * 2, [ext] * 2 + [padded] * 2, 4,
        semaphores=(2,), out_specs=[inside] * 3 + [outside] * 2,
    )(kappa, initial, before, after, left, right)
    odd = jnp.zeros(sides, jnp.float32)

    for d in several:
        bit = d & -d
        tiles[d], strips[d] = swap(tiles[d ^ bit], "tm", bit), swap(strips[d ^ bit], "tm", bit)
    near, far, last = singles[0], singles[-1], count - 1
    first, second = swap(tiles[last ^ near][:share], "tm", near), swap(tiles[last ^ far][share:], "tm", far)
    strips[last] = swap(strips[last ^ near], "tm", near)
    for d in (*singles, *several):
        if d != last:
            even, odd, tail = call(
                functools.partial(middle_kernel, grid, d), [sides, sides, ext], work, MIDDLE,
                input_output_aliases={1: 0, 2: 1, 3: 2},
            )(kap, even, odd, tail, tiles[d], strips[d])
    own = [sides, sides, ext] if count != 4 else [(1, *grid.ext), (1, *grid.ext), ext]
    c_new, f_new = call(
        functools.partial(last_kernel, grid, count), [c_guess.shape] * 2, work + [padded] + [(rows, width)] * 2 + own, 8,
        semaphores=(2, len(CHUNKS)), input_output_aliases={7: 0, 8: 1},
        in_specs=[inside] * 7 + [outside] * 2, out_specs=[outside] * 2,
    )(kap, even, odd, tail, first, second, strips[last], c_new, f_new)
    return c_new, f_new


def solution(mesh):
    return jax.shard_map(
        on_device,
        mesh=mesh,
        in_specs=(P("sx", "sy"), P("sx", "sy"), P("tm", "sx", "sy")),
        out_specs=(P("tm", "sx", "sy"), P("tm", "sx", "sy")),
        check_vma=False,
    )
```
